512 devices in a mesh: rows: 32 (over y, x), cols: 16 (over z, core).
Axes of the slice: x: 4, y: 8, z: 8, core: 2. Of those that a mesh axis runs over, the one named last changes fastest.
Arguments:
- source_cells: float32 [64, 32768], P(None, 'rows'), may hold values from -4.5 to 4.5
- target_cells: float32 [64, 32768], P(None, 'cols'), may hold values from -4.5 to 4.5
- source_mass: float32 [32768], P('rows'), may hold values from 0.2 to 15, as said below
- target_mass: float32 [32768], P('cols'), may hold values from 0.2 to 15, as said below
Outputs:
- source_potential: float32 [32768], P('rows')
- target_potential: float32 [32768], P('cols')
- source_map: float32 [64, 32768], P(None, ('rows', 'cols'))
- target_map: float32 [64, 32768], P(None, 'cols')
The draws below stay inside these ranges and needn't reach their ends.
Inputs may be any that keep to these rules, and one draw needn't show every extreme that they name: `source_mass`: positive weights. `target_mass`: positive weights.
All inputs are finite; a program needn't handle non-finite values.
Results may differ from the reference program's by a relative error of at most 0.0003.
Values sent between devices are 32-bit elements; how exact they have to be, the bound alone decides.
A program may use at most 128 MiB of HBM per device.

```python
import jax
import jax.numpy as jnp
from jax import lax

DIMS = 64
ITERS = 2
SRC_DEV = 1024
TGT_DEV = 2048
NS = 32768
NT = 32768
N_ROWS = 32
N_COLS = 16


def outlier_cells(base, count, flag_key, level_key, sign):
    picks = jax.random.randint(flag_key, (count // 32,), 0, 32)
    places = jnp.arange(count, dtype=jnp.int32)
    flags = (places % 32 == jnp.repeat(picks, 32)).astype(jnp.float32)
    levels = jax.random.randint(level_key, (count,), 0, 3).astype(jnp.float32)
    offsets = sign * flags * (2.5 + 0.5 * levels)
    shrink = 1.0 - 0.75 * flags
    return base * shrink[None, :] + offsets[None, :]


def draw_source_cells(key, part):
    key = jax.random.fold_in(key, 11)
    first_key, flag_key, level_key = jax.random.split(key, 3)
    base = jnp.clip(0.35 * jax.random.normal(first_key, (DIMS, NS), jnp.float32), -2.0, 2.0)
    return outlier_cells(base, NS, flag_key, level_key, 1.0)


def draw_target_cells(key, part):
    key = jax.random.fold_in(key, 17)
    first_key, flag_key, level_key = jax.random.split(key, 3)
    base = jnp.clip(0.35 * jax.random.normal(first_key, (DIMS, NT), jnp.float32), -2.0, 2.0)
    return outlier_cells(base, NT, flag_key, level_key, -1.0)


def draw_source_mass(key, part):
    key = jax.random.fold_in(key, 23)
    spread = 1.2
    values = jax.random.uniform(key, (NS,), jnp.float32, -spread, spread)
    places = jnp.arange(NS, dtype=jnp.float32) / (NS - 1)
    return jnp.exp(values) * (1.0 + 2.0 * places)


def draw_target_mass(key, part):
    key = jax.random.fold_in(key, 29)
    spread = 1.2
    values = jax.random.uniform(key, (NT,), jnp.float32, -spread, spread)
    places = jnp.arange(NT, dtype=jnp.float32) / (NT - 1)
    return jnp.exp(values) * (1.0 + 2.0 * places)


def setup_inputs(seed: int = 0) -> dict:
    keys = jax.random.split(jax.random.key(seed), 5)
    source_cells = draw_source_cells(jax.random.fold_in(keys[4], 71), 0)
    target_cells = draw_target_cells(jax.random.fold_in(keys[4], 71), 0)
    source_mass = draw_source_mass(jax.random.fold_in(keys[4], 71), 0)
    target_mass = draw_target_mass(jax.random.fold_in(keys[4], 71), 0)
    return dict(source_cells=source_cells, target_cells=target_cells, source_mass=source_mass, target_mass=target_mass)


SMOOTHING = 0.5
PRECISE = lax.Precision.HIGHEST


def cost_block(left_points, right_points, left_norms, right_norms):
    inner = lax.dot_general(left_points, right_points, (((0,), (0,)), ((), ())), precision=PRECISE, preferred_element_type=jnp.float32)
    return (left_norms[:, None] + right_norms[None, :]) - 2.0 * inner


def reference(source_cells, target_cells, source_mass, target_mass):
    source_log = jnp.log(source_mass) - jnp.log(jnp.sum(source_mass))
    target_log = jnp.log(target_mass) - jnp.log(jnp.sum(target_mass))
    source_norms = jnp.sum(source_cells * source_cells, axis=0)
    target_norms = jnp.sum(target_cells * target_cells, axis=0)
    source_blocks = source_cells.reshape(DIMS, N_ROWS, SRC_DEV).transpose(1, 0, 2)
    source_norm_blocks = source_norms.reshape(N_ROWS, SRC_DEV)
    target_blocks = target_cells.reshape(DIMS, N_COLS, TGT_DEV).transpose(1, 0, 2)
    target_norm_blocks = target_norms.reshape(N_COLS, TGT_DEV)
    target_pot = jnp.zeros((NT,), jnp.float32)
    source_pot = jnp.zeros((NS,), jnp.float32)
    for iteration in range(ITERS):
        def row_lse(element):
            points, norms = element
            scores = (target_pot[None, :] - cost_block(points, target_cells, norms, target_norms)) / SMOOTHING
            maximum = jnp.max(scores, axis=1)
            return maximum + jnp.log(jnp.sum(jnp.exp(scores - maximum[:, None]), axis=1))

        source_pot = SMOOTHING * source_log - SMOOTHING * lax.map(row_lse, (source_blocks, source_norm_blocks)).reshape(-1)

        def column_lse(element):
            points, norms = element
            scores = (source_pot[:, None] - cost_block(source_cells, points, source_norms, norms)) / SMOOTHING
            maximum = jnp.max(scores, axis=0)
            return maximum + jnp.log(jnp.sum(jnp.exp(scores - maximum[None, :]), axis=0))

        target_pot = SMOOTHING * target_log - SMOOTHING * lax.map(column_lse, (target_blocks, target_norm_blocks)).reshape(-1)

    def source_image(element):
        points, norms, potential = element
        coupling = jnp.exp((potential[:, None] + target_pot[None, :] - cost_block(points, target_cells, norms, target_norms)) / SMOOTHING)
        numerator = lax.dot_general(target_cells, coupling, (((1,), (1,)), ((), ())), precision=PRECISE, preferred_element_type=jnp.float32)
        return numerator / jnp.sum(coupling, axis=1)[None, :]

    source_map = lax.map(source_image, (source_blocks, source_norm_blocks, source_pot.reshape(N_ROWS, SRC_DEV)))
    source_map = source_map.transpose(1, 0, 2).reshape(DIMS, NS)

    def target_image(element):
        points, norms, potential = element
        coupling = jnp.exp((source_pot[:, None] + potential[None, :] - cost_block(source_cells, points, source_norms, norms)) / SMOOTHING)
        numerator = jnp.dot(source_cells, coupling, precision=PRECISE, preferred_element_type=jnp.float32)
        return numerator / jnp.sum(coupling, axis=0)[None, :]

    target_map = lax.map(target_image, (target_blocks, target_norm_blocks, target_pot.reshape(N_COLS, TGT_DEV)))
    target_map = target_map.transpose(1, 0, 2).reshape(DIMS, NT)
    return source_pot, target_pot, source_map, target_map
```

```python
import functools
import math

import jax
import jax.numpy as jnp
from jax import lax
from jax.experimental import pallas as pl
from jax.experimental.pallas import tpu as pltpu
from jax.sharding import PartitionSpec as P

MESH = pl.DeviceIdType.MESH
F32 = jnp.float32
BF16 = jnp.bfloat16
LOG2E = math.log2(math.e)
LN2 = math.log(2.0)
NEG = -3.0e38

DIMS = 64
SRC = 1024
TGT = 2048
NX, NY, NZ, NC = 4, 8, 8, 2
GROUPS = 16


def far(n, r):
    return min(r, n - r)


XY_OFFSETS = sorted(
    [(dy, dx) for dy in range(NY) for dx in range(NX) if dy or dx],
    key=lambda o: -(far(NY, o[0]) + far(NX, o[1])),
)
ZC_OFFSETS = sorted(
    [(dz, dc) for dz in range(NZ) for dc in range(NC) if dz or dc],
    key=lambda o: -(far(NZ, o[0]) + 0.3 * o[1]),
)
Y_OFFSETS = sorted(range(1, NY), key=lambda r: -far(NY, r))
X_OFFSETS = sorted(range(1, NX), key=lambda r: -far(NX, r))
Z_OFFSETS = sorted(range(1, NZ), key=lambda r: -far(NZ, r))


def split3(value):
    high = value.astype(BF16)
    rest = value - high.astype(F32)
    middle = rest.astype(BF16)
    low = (rest - middle.astype(F32)).astype(BF16)
    return high, middle, low


def split2(value):
    high = value.astype(BF16)
    return high, (value - high.astype(F32)).astype(BF16)


def fold_rows(value, op):
    rows = value.shape[0]
    while rows > 8:
        rows //= 2
        value = op(value[:rows], value[rows:])
    return value


def to_row(ref, groups):
    return jnp.concatenate([ref[r : r + 1, :] for r in range(groups)], axis=1)


def from_row(ref, value, groups):
    for r in range(groups):
        ref[r : r + 1, :] = value[:, r * 128 : (r + 1) * 128]


def kernel(
    x_ref, y_ref, a_ref, b_ref,
    f_ref, g_ref, smap_ref, tmap_ref,
    xt, yk, t, ehi, elo, fb, part,
    f1_out, f1_in, f2_out, f2_in, g1_out, g1_in, g2_out, g2_in,
    sa_out, sa_in, sb_out, sb_in, row,
    tn, rsx, r1, rsy, r2,
    sn, sc_in, zs, z_in, fin, fin_in,
    send, recv, ag_recv,
):
    rows_at, cols_at = lax.axis_index("rows"), lax.axis_index("cols")
    my, mx = rows_at // NX, lax.rem(rows_at, NX)
    mz, mc = cols_at // NC, lax.rem(cols_at, NC)

    def xy(dy, dx):
        return (lax.rem(my + dy, NY) * NX + lax.rem(mx + dx, NX), cols_at)

    def zc(dz, dc):
        return (rows_at, lax.rem(mz + dz, NZ) * NC + lax.rem(mc + dc, NC))

    def push(src, dst, phase, device, sem=None):
        pltpu.make_async_remote_copy(
            src_ref=src, dst_ref=dst, send_sem=send.at[phase],
            recv_sem=recv.at[phase] if sem is None else sem,
            device_id=device, device_id_type=MESH,
        ).start()

    def await_bytes(ref, sem):
        pltpu.make_async_copy(ref, ref, sem).wait()

    def push_xy(src, slots, phase):
        for dy, dx in XY_OFFSETS:
            push(src, slots.at[dy * NX + dx], phase, xy(dy, dx))

    def push_zc(src, slots, phase):
        for dz, dc in ZC_OFFSETS:
            push(src, slots.at[dz * NC + dc], phase, zc(dz, dc))

    barrier = pltpu.get_barrier_semaphore()
    for dy, dx in XY_OFFSETS:
        pl.semaphore_signal(barrier, inc=1, device_id=xy(dy, dx), device_id_type=MESH)
    for dz, dc in ZC_OFFSETS:
        pl.semaphore_signal(barrier, inc=1, device_id=zc(dz, dc), device_id_type=MESH)

    x = x_ref[...]
    xs = x * (4.0 * LOG2E)
    xh, xm, xl = split3(xs)
    xt[:, 0:128] = jnp.concatenate([xh.astype(F32), xm.astype(F32)], axis=0).T.astype(BF16)
    xt[:, 128:256] = xt[:, 0:128]
    xt[:, 256:384] = jnp.concatenate([xh.astype(F32), xl.astype(F32)], axis=0).T.astype(BF16)
    xt[:, 384:512] = jnp.where(lax.broadcasted_iota(jnp.int32, (SRC, 128), 1) < 3, 1.0, 0.0).astype(BF16)
    y = y_ref[...]
    yh, ym, yl = split3(y)
    yk[0:64, :] = yh
    yk[64:128, :] = yh
    yk[128:192, :] = ym
    yk[192:256, :] = ym
    yk[256:320, :] = yl
    yk[320:384, :] = yh
    ny = jnp.sum(y * y, axis=0, keepdims=True) * (-2.0 * LOG2E)
    nh, nm, nl = split3(ny)
    pick = lax.broadcasted_iota(jnp.int32, (128, TGT), 0)
    norms = jnp.where(
        pick == 0, nh.astype(F32), jnp.where(pick == 1, nm.astype(F32), jnp.where(pick == 2, nl.astype(F32), 0.0))
    )
    yk[384:512, :] = norms.astype(BF16)

    def first(k, _):
        at = pl.ds(pl.multiple_of(k * 128, 128), 128)
        t[at, :] = jnp.dot(xt[at, :], yk[...], preferred_element_type=F32)
        highest = t[at, 0:128]
        for g in range(1, GROUPS):
            highest = jnp.maximum(highest, t[at, g * 128 : (g + 1) * 128])
        total = jnp.exp2(t[at, 0:128] - highest)
        for g in range(1, GROUPS):
            total += jnp.exp2(t[at, g * 128 : (g + 1) * 128] - highest)
        highest, total = highest.T, total.T
        top = jnp.max(highest, axis=0, keepdims=True)
        summed = jnp.sum(total * jnp.exp2(highest - top), axis=0, keepdims=True)
        f1_out[pl.ds(k, 1), :] = top + jnp.log(summed) * LOG2E
        return 0

    lax.fori_loop(0, 8, first, 0)
    sa_out[...] = jnp.broadcast_to(jnp.sum(a_ref[...], axis=(0, 1), keepdims=True), (1, 128))
    sb_out[...] = jnp.broadcast_to(jnp.sum(b_ref[...], axis=(0, 1), keepdims=True), (1, 128))

    pl.semaphore_wait(barrier, len(XY_OFFSETS) + len(ZC_OFFSETS))
    push_zc(f1_out, f1_in, 0)
    push_xy(sa_out, sa_in, 1)
    push_zc(sb_out, sb_in, 2)

    f1_in[0] = f1_out[...]
    await_bytes(f1_in.at[pl.ds(1, 15)], recv.at[0])
    highest = jnp.max(f1_in[...], axis=0)
    summed = jnp.sum(jnp.exp2(f1_in[...] - highest[None]), axis=0)
    log_a = jnp.log(a_ref[...]) * LOG2E
    first_f = log_a - (highest + jnp.log(summed) * LOG2E)
    row[0:8, :] = first_f
    for r in range(8):
        fb[r * 128 : (r + 1) * 128, :] = jnp.broadcast_to(row[r : r + 1, :], (128, 128)).T

    WIDE = 512
    for c in range(TGT // WIDE):
        cs = slice(c * WIDE, (c + 1) * WIDE)

        def shifted(k, top):
            at = pl.ds(pl.multiple_of(k * 64, 64), 64)
            f = fb[at, :]
            value = t[at, cs] + jnp.concatenate([f] * (WIDE // 128), axis=1)
            t[at, cs] = value
            return jnp.maximum(top, fold_rows(value, jnp.maximum))

        top = lax.fori_loop(0, 16, shifted, jnp.full((8, WIDE), NEG, F32), unroll=2)
        top = jnp.max(top, axis=0, keepdims=True)

        def powers(k, total):
            at = pl.ds(pl.multiple_of(k * 64, 64), 64)
            e = jnp.exp2(t[at, cs] - top)
            t[at, cs] = e
            high, low = split2(e)
            ehi[at, cs] = high
            elo[at, cs] = low
            return total + fold_rows(e, jnp.add)

        total = lax.fori_loop(0, 16, powers, jnp.zeros((8, WIDE), F32), unroll=2)
        total = jnp.sum(total, axis=0, keepdims=True)
        logs = top + jnp.log(total) * LOG2E
        for r in range(WIDE // 128):
            at = c * (WIDE // 128) + r
            g1_out[at : at + 1, :] = logs[:, r * 128 : (r + 1) * 128]
            row[8 + at : 9 + at, :] = top[:, r * 128 : (r + 1) * 128]
    push_xy(g1_out, g1_in, 3)
    g1_in[0] = g1_out[...]
    await_bytes(g1_in.at[pl.ds(1, 31)], recv.at[3])
    highest = jnp.max(g1_in[...], axis=0)
    summed = jnp.sum(jnp.exp2(g1_in[...] - highest[None]), axis=0)
    b = b_ref[...]
    first_g = jnp.log(b) * LOG2E - (highest + jnp.log(summed) * LOG2E)
    row[8:24, :] = jnp.exp2(row[8:24, :] + first_g)
    scale = to_row(row.at[8:24, :], 16)

    def weighted(k, _):
        at = pl.ds(pl.multiple_of(k * 64, 64), 64)
        total = t[at, 0:128] * scale[:, 0:128]
        for g in range(1, GROUPS):
            gs = slice(g * 128, (g + 1) * 128)
            total += t[at, gs] * scale[:, gs]
        part[at, :] = total
        return 0

    lax.fori_loop(0, 16, weighted, 0, unroll=2)
    for r in range(8):
        f2_out[r : r + 1, :] = jnp.sum(part[r * 128 : (r + 1) * 128, :].T, axis=0, keepdims=True)
    push_zc(f2_out, f2_in, 4)
    f2_in[0] = f2_out[...]
    nx = jnp.sum(x * x, axis=0, keepdims=True) * (2.0 * LOG2E)
    from_row(row.at[24:32, :], nx, 8)
    await_bytes(f2_in.at[pl.ds(1, 15)], recv.at[4])
    sums = jnp.sum(f2_in[...], axis=0)
    ratio = a_ref[...] / sums
    row[32:40, :] = ratio
    u = to_row(row.at[32:40, :], 8)

    def stacked(points, weights):
        high, low = split2(points * weights)
        wh, wl = split2(weights)
        tail = lax.broadcasted_iota(jnp.int32, (16, weights.shape[1]), 0)
        pair = jnp.where(tail == 0, wh.astype(F32), jnp.where(tail == 1, wl.astype(F32), 0.0))
        return jnp.concatenate([high, low, pair.astype(BF16)], axis=0)

    xu = stacked(x, u)
    for c in range(4):
        cs = slice(c * 512, (c + 1) * 512)
        one = jnp.dot(xu, ehi[:, cs], preferred_element_type=F32)
        two = jnp.dot(xu, elo[:, cs], preferred_element_type=F32)
        w = scale[:, cs]
        tn[:, cs] = (one[0:64] + one[64:128] + two[0:64]) * w
        mass = (one[128:129] + one[129:130] + two[128:129]) * w
        for r in range(4):
            g2_out[c * 4 + r : c * 4 + r + 1, :] = mass[:, r * 128 : (r + 1) * 128]
    push_xy(g2_out, g2_in, 5)
    for dx in X_OFFSETS:
        at = pl.multiple_of(lax.rem(mx + dx, NX) * 512, 512)
        push(tn.at[:, pl.ds(at, 512)], rsx.at[dx], 6, xy(0, dx))
    g2_in[0] = g2_out[...]
    await_bytes(g2_in.at[pl.ds(1, 31)], recv.at[5])
    mass = jnp.sum(g2_in[...], axis=0)
    ratio_g = b / mass
    row[40:56, :] = row[8:24, :] * ratio_g
    row[56:72, :] = mass
    q = to_row(row.at[40:56, :], 16)

    await_bytes(rsx.at[pl.ds(1, 3)], recv.at[6])
    own = pl.ds(pl.multiple_of(mx * 512, 512), 512)
    r1[...] = tn[:, own] + rsx[1] + rsx[2] + rsx[3]

    def y_piece(position):
        half, group = lax.rem(position, 2), position // 2
        return (
            pl.ds(pl.multiple_of(half * 32, 32), 32),
            pl.ds(pl.multiple_of(group * 128, 128), 128),
        )

    for dy in Y_OFFSETS:
        halves, groups = y_piece(lax.rem(my + dy, NY))
        push(r1.at[halves, groups], rsy.at[dy], 7, xy(dy, 0))

    yq = stacked(y, q)
    nt = (((1,), (1,)), ((), ()))
    for c in range(4):
        rs = slice(c * 256, (c + 1) * 256)
        one = lax.dot_general(yq, ehi[rs, :], nt, preferred_element_type=F32)
        two = lax.dot_general(yq, elo[rs, :], nt, preferred_element_type=F32)
        sn[0, :, rs] = one[0:32] + one[64:96] + two[0:32]
        sn[1, :, rs] = one[32:64] + one[96:128] + two[32:64]
        weight = one[128:129] + one[129:130] + two[128:129]
        sn[2, :, rs] = jnp.broadcast_to(weight, (32, 256))
    partner = zc(0, 1)
    push(sn.at[1 - mc], sc_in.at[pl.ds(0, 32)], 8, partner)
    push(sn.at[2, pl.ds(0, 8)], sc_in.at[pl.ds(32, 8)], 8, partner)
    await_bytes(sc_in, recv.at[8])
    for k in range(NZ):
        ks = slice(k * 128, (k + 1) * 128)
        zs[k, 0:32, :] = sn[mc, :, ks] + sc_in[0:32, ks]
        zs[k, 32:40, :] = sn[2, 0:8, ks] + sc_in[32:40, ks]
    for dz in Z_OFFSETS:
        push(zs.at[lax.rem(mz + dz, NZ)], z_in.at[dz], 9, zc(dz, 0))

    await_bytes(rsy.at[pl.ds(1, 7)], recv.at[7])
    halves, groups = y_piece(my)
    own_sum = r1[halves, groups]
    for k in range(1, NY):
        own_sum += rsy[k]
    mass_at = 56 + mx * 4 + my // 2
    r2[...] = own_sum / row[pl.ds(mass_at, 1), :]
    out_rows = halves
    out_cols = pl.ds(pl.multiple_of(mx * 512 + (my // 2) * 128, 128), 128)
    for dy in Y_OFFSETS:
        push(r2, tmap_ref.at[out_rows, out_cols], 10, xy(dy, 0))
    tmap_ref[out_rows, out_cols] = r2[...]

    await_bytes(z_in.at[pl.ds(1, 7)], recv.at[9])
    own_sum = zs[mz]
    for k in range(1, NZ):
        own_sum += z_in[k]
    fin[...] = own_sum[0:32] / own_sum[32:33]
    push(fin, fin_in, 11, partner)

    await_bytes(rsy.at[pl.ds(1, 7)], recv.at[10])
    for dx in X_OFFSETS:
        push(tmap_ref.at[:, own], tmap_ref.at[:, own], 12, xy(0, dx))

    sa_in[0] = sa_out[...]
    sb_in[0] = sb_out[...]
    await_bytes(sa_in.at[pl.ds(1, 31)], recv.at[1])
    await_bytes(sb_in.at[pl.ds(1, 15)], recv.at[2])
    log_sa = jnp.log(jnp.sum(sa_in[...], axis=0))
    log_sb = jnp.log(jnp.sum(sb_in[...], axis=0))
    f_ref[...] = (0.5 * LN2) * (first_f + row[24:32, :]) + 0.5 * jnp.log(ratio) - (log_sa - 0.5 * log_sb)
    g_ref[...] = (0.5 * LN2) * first_g + 0.5 * jnp.log(ratio_g) - (log_sb - log_sa)

    await_bytes(fin_in, recv.at[11])
    mine, other = fin[...], fin_in[...]
    low = jnp.where(mc == 0, mine, other)
    high = jnp.where(mc == 0, other, mine)
    both = jnp.concatenate([low, high], axis=0)
    smap_ref[...] = jnp.where(mc == 0, both[:, 0:64], both[:, 64:128])

    await_bytes(rsx.at[pl.ds(1, 3)], recv.at[12])

    await_bytes(f1_in.at[pl.ds(1, 15)], send.at[0])
    await_bytes(sa_in.at[pl.ds(1, 31)], send.at[1])
    await_bytes(sb_in.at[pl.ds(1, 15)], send.at[2])
    await_bytes(g1_in.at[pl.ds(1, 31)], send.at[3])
    await_bytes(f2_in.at[pl.ds(1, 15)], send.at[4])
    await_bytes(g2_in.at[pl.ds(1, 31)], send.at[5])
    await_bytes(rsx.at[pl.ds(1, 3)], send.at[6])
    await_bytes(rsy.at[pl.ds(1, 7)], send.at[7])
    await_bytes(sc_in, send.at[8])
    await_bytes(z_in.at[pl.ds(1, 7)], send.at[9])
    await_bytes(rsy.at[pl.ds(1, 7)], send.at[10])
    await_bytes(fin_in, send.at[11])
    await_bytes(rsx.at[pl.ds(1, 3)], send.at[12])


def local(source_cells, target_cells, source_mass, target_mass):
    vmem = pl.BlockSpec(memory_space=pltpu.VMEM)
    f, g, smap, tmap = pl.pallas_call(
        kernel,
        out_shape=(
            jax.ShapeDtypeStruct((8, 128), F32),
            jax.ShapeDtypeStruct((16, 128), F32),
            jax.ShapeDtypeStruct((DIMS, 64), F32),
            jax.ShapeDtypeStruct((DIMS, TGT), F32),
        ),
        in_specs=[vmem] * 4,
        out_specs=(vmem,) * 4,
        scratch_shapes=[
            pltpu.VMEM((SRC, 512), BF16),
            pltpu.VMEM((512, TGT), BF16),
            pltpu.VMEM((SRC, TGT), F32),
            pltpu.VMEM((SRC, TGT), BF16),
            pltpu.VMEM((SRC, TGT), BF16),
            pltpu.VMEM((SRC, 128), F32),
            pltpu.VMEM((SRC, 128), F32),
            pltpu.VMEM((8, 128), F32),
            pltpu.VMEM((16, 8, 128), F32),
            pltpu.VMEM((8, 128), F32),
            pltpu.VMEM((16, 8, 128), F32),
            pltpu.VMEM((16, 128), F32),
            pltpu.VMEM((32, 16, 128), F32),
            pltpu.VMEM((16, 128), F32),
            pltpu.VMEM((32, 16, 128), F32),
            pltpu.VMEM((1, 128), F32),
            pltpu.VMEM((32, 1, 128), F32),
            pltpu.VMEM((1, 128), F32),
            pltpu.VMEM((16, 1, 128), F32),
            pltpu.VMEM((72, 128), F32),
            pltpu.VMEM((DIMS, TGT), F32),
            pltpu.VMEM((NX, DIMS, 512), F32),
            pltpu.VMEM((DIMS, 512), F32),
            pltpu.VMEM((NY, 32, 128), F32),
            pltpu.VMEM((32, 128), F32),
            pltpu.VMEM((3, 32, SRC), F32),
            pltpu.VMEM((40, SRC), F32),
            pltpu.VMEM((NZ, 40, 128), F32),
            pltpu.VMEM((NZ, 40, 128), F32),
            pltpu.VMEM((32, 128), F32),
            pltpu.VMEM((32, 128), F32),
            pltpu.SemaphoreType.DMA((13,)),
            pltpu.SemaphoreType.DMA((13,)),
            pltpu.SemaphoreType.DMA((8,)),
        ],
        compiler_params=pltpu.CompilerParams(
            collective_id=0, has_side_effects=True, vmem_limit_bytes=56 << 20
        ),
    )(source_cells, target_cells, source_mass.reshape(8, 128), target_mass.reshape(16, 128))
    return f.reshape(-1), g.reshape(-1), smap, tmap


def solution(mesh):
    in_specs = (P(None, "rows"), P(None, "cols"), P("rows"), P("cols"))
    out_specs = (P("rows"), P("cols"), P(None, ("rows", "cols")), P(None, "cols"))
    return jax.shard_map(local, mesh=mesh, in_specs=in_specs, out_specs=out_specs, check_vma=False)
```

```python
import functools
import math

import jax
import jax.numpy as jnp
from jax import lax
from jax.experimental import pallas as pl
from jax.experimental.pallas import tpu as pltpu
from jax.sharding import PartitionSpec as P

MESH = pl.DeviceIdType.MESH
F32 = jnp.float32
BF16 = jnp.bfloat16
LOG2E = math.log2(math.e)
LN2 = math.log(2.0)
NEG = -3.0e38

DIMS = 64
SRC = 1024
TGT = 2048
NX, NY, NZ, NC = 4, 8, 8, 2
GROUPS = 16


def far(n, r):
    return min(r, n - r)


XY_OFFSETS = sorted(
    [(dy, dx) for dy in range(NY) for dx in range(NX) if dy or dx],
    key=lambda o: -(far(NY, o[0]) + far(NX, o[1])),
)
ZC_OFFSETS = sorted(
    [(dz, dc) for dz in range(NZ) for dc in range(NC) if dz or dc],
    key=lambda o: -(far(NZ, o[0]) + 0.3 * o[1]),
)
Y_OFFSETS = sorted(range(1, NY), key=lambda r: -far(NY, r))
X_OFFSETS = sorted(range(1, NX), key=lambda r: -far(NX, r))
Z_OFFSETS = sorted(range(1, NZ), key=lambda r: -far(NZ, r))


def split3(value):
    high = value.astype(BF16)
    rest = value - high.astype(F32)
    middle = rest.astype(BF16)
    low = (rest - middle.astype(F32)).astype(BF16)
    return high, middle, low


def split2(value):
    high = value.astype(BF16)
    return high, (value - high.astype(F32)).astype(BF16)


def fold_rows(value, op):
    rows = value.shape[0]
    while rows > 8:
        rows //= 2
        value = op(value[:rows], value[rows:])
    return value


def to_row(ref, groups):
    return jnp.concatenate([ref[r : r + 1, :] for r in range(groups)], axis=1)


def from_row(ref, value, groups):
    for r in range(groups):
        ref[r : r + 1, :] = value[:, r * 128 : (r + 1) * 128]


def kernel(
    x_hbm, y_hbm, a_hbm, b_hbm,
    fg_hbm, smap_hbm, tmap_hbm,
    x_ref, y_ref, a_ref, b_ref, fg_ref, smap_ref, ta_ref, tb_ref,
    xt, yk, t, ehi, elo, fb, part,
    f1_out, f1_in, f2_out, f2_in, g1_out, g1a_in, g1b_in, g2_out, g2a_in, g2b_in,
    sa_out, sa_in, sb_out, sb_in, row,
    na, nb, ax_in, ra, ay_in, by_in, rb, bx_in, fin_t,
    sn, sc_in, zs, z_in, fin, fin_in,
    send, recv, near,
):
    rows_at, cols_at = lax.axis_index("rows"), lax.axis_index("cols")
    my, mx = rows_at // NX, lax.rem(rows_at, NX)
    mz, mc = cols_at // NC, lax.rem(cols_at, NC)

    def xy(dy, dx):
        return (lax.rem(my + dy, NY) * NX + lax.rem(mx + dx, NX), cols_at)

    def zc(dz, dc):
        return (rows_at, lax.rem(mz + dz, NZ) * NC + lax.rem(mc + dc, NC))

    def push(src, dst, phase, device):
        pltpu.make_async_remote_copy(
            src_ref=src, dst_ref=dst, send_sem=send.at[phase], recv_sem=recv.at[phase],
            device_id=device, device_id_type=MESH,
        ).start()

    def await_bytes(ref, sem):
        pltpu.make_async_copy(ref, ref, sem).wait()

    def push_xy(src, slots, phase):
        for dy, dx in XY_OFFSETS:
            push(src, slots.at[dy * NX + dx], phase, xy(dy, dx))

    def push_zc(src, slots, phase):
        for dz, dc in ZC_OFFSETS:
            push(src, slots.at[dz * NC + dc], phase, zc(dz, dc))

    def fetch(src, dst, k):
        copy = pltpu.make_async_copy(src, dst, near.at[k])
        copy.start()
        return copy

    loads = [
        fetch(x_hbm, x_ref, 0),
        fetch(y_hbm, y_ref, 1),
        fetch(a_hbm, a_ref, 2),
        fetch(b_hbm, b_ref, 3),
    ]
    barrier = pltpu.get_barrier_semaphore()
    for dy, dx in XY_OFFSETS:
        pl.semaphore_signal(barrier, inc=1, device_id=xy(dy, dx), device_id_type=MESH)
    for dz, dc in ZC_OFFSETS:
        pl.semaphore_signal(barrier, inc=1, device_id=zc(dz, dc), device_id_type=MESH)

    loads[0].wait()
    x = x_ref[...]
    xs = x * (4.0 * LOG2E)
    xh, xm, xl = split3(xs)
    xt[:, 0:128] = jnp.concatenate([xh.astype(F32), xm.astype(F32)], axis=0).T.astype(BF16)
    xt[:, 128:256] = xt[:, 0:128]
    xt[:, 256:384] = jnp.concatenate([xh.astype(F32), xl.astype(F32)], axis=0).T.astype(BF16)
    xt[:, 384:512] = jnp.where(lax.broadcasted_iota(jnp.int32, (SRC, 128), 1) < 3, 1.0, 0.0).astype(BF16)
    loads[1].wait()
    y = y_ref[...]
    yh, ym, yl = split3(y)
    yk[0:64, :] = yh
    yk[64:128, :] = yh
    yk[128:192, :] = ym
    yk[192:256, :] = ym
    yk[256:320, :] = yl
    yk[320:384, :] = yh
    ny = jnp.sum(y * y, axis=0, keepdims=True) * (-2.0 * LOG2E)
    nh, nm, nl = split3(ny)
    pick = lax.broadcasted_iota(jnp.int32, (16, TGT), 0)
    norms = jnp.where(
        pick == 0, nh.astype(F32), jnp.where(pick == 1, nm.astype(F32), jnp.where(pick == 2, nl.astype(F32), 0.0))
    )
    yk[384:400, :] = norms.astype(BF16)
    yk[400:512, :] = jnp.zeros((112, TGT), BF16)

    def score(k):
        at = slice(k * 128, (k + 1) * 128)
        t[at, :] = jnp.dot(xt[at, :], yk[...], preferred_element_type=F32)

    def row_logs(k):
        at = slice(k * 128, (k + 1) * 128)
        highest = t[at, 0:128]
        for g in range(1, GROUPS):
            highest = jnp.maximum(highest, t[at, g * 128 : (g + 1) * 128])
        total = jnp.exp2(t[at, 0:128] - highest)
        for g in range(1, GROUPS):
            total += jnp.exp2(t[at, g * 128 : (g + 1) * 128] - highest)
        highest, total = highest.T, total.T
        top = jnp.max(highest, axis=0, keepdims=True)
        summed = jnp.sum(total * jnp.exp2(highest - top), axis=0, keepdims=True)
        f1_out[k : k + 1, :] = top + jnp.log(summed) * LOG2E

    score(0)
    for k in range(8):
        if k < 7:
            score(k + 1)
        row_logs(k)
    loads[2].wait()
    loads[3].wait()
    sa_out[...] = jnp.broadcast_to(jnp.sum(a_ref[...], axis=(0, 1), keepdims=True), (1, 128))
    sb_out[...] = jnp.broadcast_to(jnp.sum(b_ref[...], axis=(0, 1), keepdims=True), (1, 128))

    pl.semaphore_wait(barrier, len(XY_OFFSETS) + len(ZC_OFFSETS))
    push_zc(f1_out, f1_in, 0)
    push_xy(sa_out, sa_in, 1)
    push_zc(sb_out, sb_in, 2)

    f1_in[0] = f1_out[...]
    await_bytes(f1_in.at[pl.ds(1, 15)], recv.at[0])
    highest = jnp.max(f1_in[...], axis=0)
    summed = jnp.sum(jnp.exp2(f1_in[...] - highest[None]), axis=0)
    log_a = jnp.log(a_ref[...]) * LOG2E
    first_f = log_a - (highest + jnp.log(summed) * LOG2E)
    row[0:8, :] = first_f
    for r in range(8):
        fb[r * 128 : (r + 1) * 128, :] = jnp.broadcast_to(row[r : r + 1, :], (128, 128)).T

    WIDE = 512
    for c in range(TGT // WIDE):
        cs = slice(c * WIDE, (c + 1) * WIDE)

        def shifted(k, top):
            at = pl.ds(pl.multiple_of(k * 64, 64), 64)
            f = fb[at, :]
            value = t[at, cs] + jnp.concatenate([f] * (WIDE // 128), axis=1)
            t[at, cs] = value
            return jnp.maximum(top, fold_rows(value, jnp.maximum))

        top = lax.fori_loop(0, 16, shifted, jnp.full((8, WIDE), NEG, F32), unroll=2)
        top = jnp.max(top, axis=0, keepdims=True)

        def powers(k, total):
            at = pl.ds(pl.multiple_of(k * 64, 64), 64)
            e = jnp.exp2(t[at, cs] - top)
            t[at, cs] = e
            high, low = split2(e)
            ehi[at, cs] = high
            elo[at, cs] = low
            return total + fold_rows(e, jnp.add)

        total = lax.fori_loop(0, 16, powers, jnp.zeros((8, WIDE), F32), unroll=2)
        total = jnp.sum(total, axis=0, keepdims=True)
        logs = top + jnp.log(total) * LOG2E
        for r in range(WIDE // 128):
            at = c * (WIDE // 128) + r
            g1_out[at : at + 1, :] = logs[:, r * 128 : (r + 1) * 128]
            row[8 + at : 9 + at, :] = top[:, r * 128 : (r + 1) * 128]
        if c == 1:
            push_xy(g1_out.at[0:8], g1a_in, 3)
    push_xy(g1_out.at[8:16], g1b_in, 4)
    b = b_ref[...]
    log_b = jnp.log(b) * LOG2E

    def log_sum(slots):
        highest = jnp.max(slots[...], axis=0)
        return highest + jnp.log(jnp.sum(jnp.exp2(slots[...] - highest[None]), axis=0)) * LOG2E

    g1a_in[0] = g1_out[0:8, :]
    await_bytes(g1a_in.at[pl.ds(1, 31)], recv.at[3])
    low_logs = log_sum(g1a_in)
    g1b_in[0] = g1_out[8:16, :]
    await_bytes(g1b_in.at[pl.ds(1, 31)], recv.at[4])
    first_g = log_b - jnp.concatenate([low_logs, log_sum(g1b_in)], axis=0)
    row[8:24, :] = jnp.exp2(row[8:24, :] + first_g)
    scale = to_row(row.at[8:24, :], 16)

    def weighted(k, _):
        at = pl.ds(pl.multiple_of(k * 64, 64), 64)
        total = t[at, 0:128] * scale[:, 0:128]
        for g in range(1, GROUPS):
            gs = slice(g * 128, (g + 1) * 128)
            total += t[at, gs] * scale[:, gs]
        part[at, :] = total
        return 0

    lax.fori_loop(0, 16, weighted, 0, unroll=2)
    for r in range(8):
        f2_out[r : r + 1, :] = jnp.sum(part[r * 128 : (r + 1) * 128, :].T, axis=0, keepdims=True)
    push_zc(f2_out, f2_in, 5)
    f2_in[0] = f2_out[...]
    nx = jnp.sum(x * x, axis=0, keepdims=True) * (2.0 * LOG2E)
    from_row(row.at[24:32, :], nx, 8)
    await_bytes(f2_in.at[pl.ds(1, 15)], recv.at[5])
    sums = jnp.sum(f2_in[...], axis=0)
    ratio = a_ref[...] / sums
    row[32:40, :] = ratio
    u = to_row(row.at[32:40, :], 8)

    def stacked(points, weights):
        high, low = split2(points * weights)
        wh, wl = split2(weights)
        tail = lax.broadcasted_iota(jnp.int32, (16, weights.shape[1]), 0)
        pair = jnp.where(tail == 0, wh.astype(F32), jnp.where(tail == 1, wl.astype(F32), 0.0))
        return jnp.concatenate([high, low, pair.astype(BF16)], axis=0)

    xu = stacked(x, u)
    for half in range(2):
        sums_ref = (na, nb)[half]
        for q in range(NX):
            cs = slice(q * 512 + half * 256, q * 512 + half * 256 + 256)
            one = jnp.dot(xu, ehi[:, cs], preferred_element_type=F32)
            two = jnp.dot(xu, elo[:, cs], preferred_element_type=F32)
            w = scale[:, cs]
            sums_ref[:, q * 256 : (q + 1) * 256] = (one[0:64] + one[64:128] + two[0:64]) * w
            mass = (one[128:129] + one[129:130] + two[128:129]) * w
            at = half * 8 + q * 2
            g2_out[at : at + 1, :] = mass[:, 0:128]
            g2_out[at + 1 : at + 2, :] = mass[:, 128:256]
        if half == 0:
            push_xy(g2_out.at[0:8], g2a_in, 6)
            for dx in X_OFFSETS:
                at = pl.multiple_of(lax.rem(mx + dx, NX) * 256, 256)
                push(na.at[:, pl.ds(at, 256)], ax_in.at[dx], 7, xy(0, dx))
        else:
            push_xy(g2_out.at[8:16], g2b_in, 8)
            for dy in Y_OFFSETS:
                at = pl.multiple_of(lax.rem(my + dy, NY) * 8, 8)
                push(nb.at[pl.ds(at, 8), :], by_in.at[dy], 9, xy(dy, 0))

    own_rows = pl.ds(pl.multiple_of(my * 8, 8), 8)
    own_cols = pl.ds(pl.multiple_of(mx * 256, 256), 256)
    await_bytes(ax_in.at[pl.ds(1, 3)], recv.at[7])
    ra[...] = na[:, own_cols] + ax_in[1] + ax_in[2] + ax_in[3]
    for dy in Y_OFFSETS:
        at = pl.multiple_of(lax.rem(my + dy, NY) * 8, 8)
        push(ra.at[pl.ds(at, 8), :], ay_in.at[dy], 10, xy(dy, 0))
    await_bytes(by_in.at[pl.ds(1, 7)], recv.at[9])
    total = nb[own_rows, :]
    for k in range(1, NY):
        total += by_in[k]
    rb[...] = total
    for dx in X_OFFSETS:
        at = pl.multiple_of(lax.rem(mx + dx, NX) * 256, 256)
        push(rb.at[:, pl.ds(at, 256)], bx_in.at[dx], 11, xy(0, dx))

    g2a_in[0] = g2_out[0:8, :]
    g2b_in[0] = g2_out[8:16, :]
    await_bytes(g2a_in.at[pl.ds(1, 31)], recv.at[6])
    row[40:48, :] = jnp.sum(g2a_in[...], axis=0)
    await_bytes(g2b_in.at[pl.ds(1, 31)], recv.at[8])
    row[48:56, :] = jnp.sum(g2b_in[...], axis=0)
    for q in range(NX):
        row[56 + q * 4 : 58 + q * 4, :] = row[40 + q * 2 : 42 + q * 2, :]
        row[58 + q * 4 : 60 + q * 4, :] = row[48 + q * 2 : 50 + q * 2, :]
    ratio_g = b / row[56:72, :]
    row[72:88, :] = row[8:24, :] * ratio_g
    weights = to_row(row.at[72:88, :], 16)

    yq = stacked(y, weights)
    nt = (((1,), (1,)), ((), ()))
    for c in range(4):
        rs = slice(c * 256, (c + 1) * 256)
        one = lax.dot_general(yq, ehi[rs, :], nt, preferred_element_type=F32)
        two = lax.dot_general(yq, elo[rs, :], nt, preferred_element_type=F32)
        sn[0, :, rs] = one[0:32] + one[64:96] + two[0:32]
        sn[1, :, rs] = one[32:64] + one[96:128] + two[32:64]
        weight = one[128:129] + one[129:130] + two[128:129]
        sn[2, :, rs] = jnp.broadcast_to(weight, (32, 256))
    partner = zc(0, 1)
    push(sn.at[1 - mc], sc_in.at[pl.ds(0, 32)], 12, partner)
    push(sn.at[2, pl.ds(0, 8)], sc_in.at[pl.ds(32, 8)], 12, partner)

    def mass_of(first):
        return jnp.concatenate([row[pl.ds(first + mx * 2, 1), :], row[pl.ds(first + mx * 2 + 1, 1), :]], axis=1)

    await_bytes(ay_in.at[pl.ds(1, 7)], recv.at[10])
    total = ra[own_rows, :]
    for k in range(1, NY):
        total += ay_in[k]
    fin_t[0] = total / mass_of(40)
    for dy in Y_OFFSETS:
        push(fin_t.at[0], ta_ref.at[own_rows, own_cols], 13, xy(dy, 0))
    await_bytes(bx_in.at[pl.ds(1, 3)], recv.at[11])
    fin_t[1] = (rb[:, own_cols] + bx_in[1] + bx_in[2] + bx_in[3]) / mass_of(48)
    for dx in X_OFFSETS:
        push(fin_t.at[1], tb_ref.at[own_rows, own_cols], 14, xy(0, dx))
    ta_ref[own_rows, own_cols] = fin_t[0]
    tb_ref[own_rows, own_cols] = fin_t[1]

    await_bytes(sc_in, recv.at[12])
    for k in range(NZ):
        ks = slice(k * 128, (k + 1) * 128)
        zs[k, 0:32, :] = sn[mc, :, ks] + sc_in[0:32, ks]
        zs[k, 32:40, :] = sn[2, 0:8, ks] + sc_in[32:40, ks]
    for dz in Z_OFFSETS:
        push(zs.at[lax.rem(mz + dz, NZ)], z_in.at[dz], 15, zc(dz, 0))

    await_bytes(bx_in.at[pl.ds(1, 3)], recv.at[14])
    for dy in Y_OFFSETS:
        push(tb_ref.at[own_rows, :], tb_ref.at[own_rows, :], 16, xy(dy, 0))
    await_bytes(ay_in.at[pl.ds(1, 7)], recv.at[13])
    for dx in X_OFFSETS:
        push(ta_ref.at[:, own_cols], ta_ref.at[:, own_cols], 17, xy(0, dx))

    sa_in[0] = sa_out[...]
    sb_in[0] = sb_out[...]
    await_bytes(sa_in.at[pl.ds(1, 31)], recv.at[1])
    await_bytes(sb_in.at[pl.ds(1, 15)], recv.at[2])
    log_sa = jnp.log(jnp.sum(sa_in[...], axis=0))
    log_sb = jnp.log(jnp.sum(sb_in[...], axis=0))
    fg_ref[0:8, :] = (0.5 * LN2) * (first_f + row[24:32, :]) + 0.5 * jnp.log(ratio) - (log_sa - 0.5 * log_sb)
    fg_ref[8:24, :] = (0.5 * LN2) * first_g + 0.5 * jnp.log(ratio_g) - (log_sb - log_sa)
    stores = [fetch(fg_ref, fg_hbm, 4)]

    await_bytes(z_in.at[pl.ds(1, 7)], recv.at[15])
    total = zs[mz]
    for k in range(1, NZ):
        total += z_in[k]
    fin[...] = total[0:32] / total[32:33]
    push(fin, fin_in, 18, partner)
    await_bytes(fin_in, recv.at[18])
    mine, other = fin[...], fin_in[...]
    low = jnp.where(mc == 0, mine, other)
    high = jnp.where(mc == 0, other, mine)
    both = jnp.concatenate([low, high], axis=0)
    smap_ref[...] = jnp.where(mc == 0, both[:, 0:64], both[:, 64:128])
    stores.append(fetch(smap_ref, smap_hbm, 5))

    await_bytes(ax_in.at[pl.ds(1, 3)], recv.at[17])
    for q in range(NX):
        stores.append(fetch(ta_ref.at[:, q * 256 : q * 256 + 256], tmap_hbm.at[:, q * 512 : q * 512 + 256], 6 + q))
    await_bytes(by_in.at[pl.ds(1, 7)], recv.at[16])
    for q in range(NX):
        stores.append(fetch(tb_ref.at[:, q * 256 : q * 256 + 256], tmap_hbm.at[:, q * 512 + 256 : q * 512 + 512], 10 + q))

    await_bytes(f1_in.at[pl.ds(1, 15)], send.at[0])
    await_bytes(sa_in.at[pl.ds(1, 31)], send.at[1])
    await_bytes(sb_in.at[pl.ds(1, 15)], send.at[2])
    await_bytes(g1a_in.at[pl.ds(1, 31)], send.at[3])
    await_bytes(g1b_in.at[pl.ds(1, 31)], send.at[4])
    await_bytes(f2_in.at[pl.ds(1, 15)], send.at[5])
    await_bytes(g2a_in.at[pl.ds(1, 31)], send.at[6])
    await_bytes(ax_in.at[pl.ds(1, 3)], send.at[7])
    await_bytes(g2b_in.at[pl.ds(1, 31)], send.at[8])
    await_bytes(by_in.at[pl.ds(1, 7)], send.at[9])
    await_bytes(ay_in.at[pl.ds(1, 7)], send.at[10])
    await_bytes(bx_in.at[pl.ds(1, 3)], send.at[11])
    await_bytes(sc_in, send.at[12])
    await_bytes(ay_in.at[pl.ds(1, 7)], send.at[13])
    await_bytes(bx_in.at[pl.ds(1, 3)], send.at[14])
    await_bytes(z_in.at[pl.ds(1, 7)], send.at[15])
    await_bytes(by_in.at[pl.ds(1, 7)], send.at[16])
    await_bytes(ax_in.at[pl.ds(1, 3)], send.at[17])
    await_bytes(fin_in, send.at[18])
    for copy in stores:
        copy.wait()


def finish(fg, sm, tm, f_hbm, g_hbm, smap_hbm, tmap_hbm, fg_v, sm_v, tm_v, come, go):
    loads = [pltpu.make_async_copy(tm.at[k * 32 : k * 32 + 32], tm_v.at[k * 32 : k * 32 + 32], come.at[k]) for k in range(2)]
    loads += [pltpu.make_async_copy(sm, sm_v, come.at[2]), pltpu.make_async_copy(fg, fg_v, come.at[3])]
    stores = [pltpu.make_async_copy(tm_v.at[k * 32 : k * 32 + 32], tmap_hbm.at[k * 32 : k * 32 + 32], go.at[k]) for k in range(2)]
    stores += [
        pltpu.make_async_copy(sm_v, smap_hbm, go.at[2]),
        pltpu.make_async_copy(fg_v.at[0:8], f_hbm, go.at[3]),
        pltpu.make_async_copy(fg_v.at[8:24], g_hbm, go.at[4]),
    ]
    for copy in loads:
        copy.start()
    for k, copy in enumerate(loads):
        copy.wait()
        stores[k].start()
    stores[4].start()
    for copy in stores:
        copy.wait()


def local(source_cells, target_cells, source_mass, target_mass):
    anywhere = pl.BlockSpec(memory_space=pl.ANY)
    results = pl.pallas_call(
        kernel,
        out_shape=(
            jax.ShapeDtypeStruct((24, 128), F32),
            jax.ShapeDtypeStruct((DIMS, 64), F32),
            jax.ShapeDtypeStruct((DIMS, TGT), F32),
        ),
        in_specs=[anywhere] * 4,
        out_specs=(anywhere,) * 3,
        scratch_shapes=[
            pltpu.VMEM((DIMS, SRC), F32),
            pltpu.VMEM((DIMS, TGT), F32),
            pltpu.VMEM((8, 128), F32),
            pltpu.VMEM((16, 128), F32),
            pltpu.VMEM((24, 128), F32),
            pltpu.VMEM((DIMS, 64), F32),
            pltpu.VMEM((DIMS, SRC), F32),
            pltpu.VMEM((DIMS, SRC), F32),
            pltpu.VMEM((SRC, 512), BF16),
            pltpu.VMEM((512, TGT), BF16),
            pltpu.VMEM((SRC, TGT), F32),
            pltpu.VMEM((SRC, TGT), BF16),
            pltpu.VMEM((SRC, TGT), BF16),
            pltpu.VMEM((SRC, 128), F32),
            pltpu.VMEM((SRC, 128), F32),
            pltpu.VMEM((8, 128), F32),
            pltpu.VMEM((16, 8, 128), F32),
            pltpu.VMEM((8, 128), F32),
            pltpu.VMEM((16, 8, 128), F32),
            pltpu.VMEM((16, 128), F32),
            pltpu.VMEM((32, 8, 128), F32),
            pltpu.VMEM((32, 8, 128), F32),
            pltpu.VMEM((16, 128), F32),
            pltpu.VMEM((32, 8, 128), F32),
            pltpu.VMEM((32, 8, 128), F32),
            pltpu.VMEM((1, 128), F32),
            pltpu.VMEM((32, 1, 128), F32),
            pltpu.VMEM((1, 128), F32),
            pltpu.VMEM((16, 1, 128), F32),
            pltpu.VMEM((88, 128), F32),
            pltpu.VMEM((DIMS, SRC), F32),
            pltpu.VMEM((DIMS, SRC), F32),
            pltpu.VMEM((NX, DIMS, 256), F32),
            pltpu.VMEM((DIMS, 256), F32),
            pltpu.VMEM((NY, 8, 256), F32),
            pltpu.VMEM((NY, 8, SRC), F32),
            pltpu.VMEM((8, SRC), F32),
            pltpu.VMEM((NX, 8, 256), F32),
            pltpu.VMEM((2, 8, 256), F32),
            pltpu.VMEM((3, 32, SRC), F32),
            pltpu.VMEM((40, SRC), F32),
            pltpu.VMEM((NZ, 40, 128), F32),
            pltpu.VMEM((NZ, 40, 128), F32),
            pltpu.VMEM((32, 128), F32),
            pltpu.VMEM((32, 128), F32),
            pltpu.SemaphoreType.DMA((19,)),
            pltpu.SemaphoreType.DMA((19,)),
            pltpu.SemaphoreType.DMA((14,)),
        ],
        compiler_params=pltpu.CompilerParams(
            collective_id=0, has_side_effects=True, vmem_limit_bytes=60 << 20
        ),
    )(source_cells, target_cells, source_mass.reshape(8, 128), target_mass.reshape(16, 128))
    f, g, smap, tmap = pl.pallas_call(
        finish,
        out_shape=(
            jax.ShapeDtypeStruct((8, 128), F32),
            jax.ShapeDtypeStruct((16, 128), F32),
            jax.ShapeDtypeStruct((DIMS, 64), F32),
            jax.ShapeDtypeStruct((DIMS, TGT), F32),
        ),
        in_specs=[anywhere] * 3,
        out_specs=(anywhere,) * 4,
        scratch_shapes=[
            pltpu.VMEM((24, 128), F32),
            pltpu.VMEM((DIMS, 64), F32),
            pltpu.VMEM((DIMS, TGT), F32),
            pltpu.SemaphoreType.DMA((4,)),
            pltpu.SemaphoreType.DMA((5,)),
        ],
    )(*results)
    return f.reshape(-1), g.reshape(-1), smap, tmap


def solution(mesh):
    in_specs = (P(None, "rows"), P(None, "cols"), P("rows"), P("cols"))
    out_specs = (P("rows"), P("cols"), P(None, ("rows", "cols")), P(None, "cols"))
    return jax.shard_map(local, mesh=mesh, in_specs=in_specs, out_specs=out_specs, check_vma=False)
```

```python
import functools
import math

import jax
import jax.numpy as jnp
from jax import lax
from jax.experimental import pallas as pl
from jax.experimental.pallas import tpu as pltpu
from jax.sharding import PartitionSpec as P

MESH = pl.DeviceIdType.MESH
F32 = jnp.float32
BF16 = jnp.bfloat16
LOG2E = math.log2(math.e)
LN2 = math.log(2.0)
NEG = -3.0e38

DIMS = 64
SRC = 1024
TGT = 2048
NX, NY, NZ, NC = 4, 8, 8, 2
GROUPS = 16


def far(n, r):
    return min(r, n - r)


XY_OFFSETS = sorted(
    [(dy, dx) for dy in range(NY) for dx in range(NX) if dy or dx],
    key=lambda o: -(far(NY, o[0]) + far(NX, o[1])),
)
ZC_OFFSETS = sorted(
    [(dz, dc) for dz in range(NZ) for dc in range(NC) if dz or dc],
    key=lambda o: -(far(NZ, o[0]) + 0.3 * o[1]),
)
Y_OFFSETS = sorted(range(1, NY), key=lambda r: -far(NY, r))
X_OFFSETS = sorted(range(1, NX), key=lambda r: -far(NX, r))
Z_OFFSETS = sorted(range(1, NZ), key=lambda r: -far(NZ, r))


def split3(value):
    high = value.astype(BF16)
    rest = value - high.astype(F32)
    middle = rest.astype(BF16)
    low = (rest - middle.astype(F32)).astype(BF16)
    return high, middle, low


def split2(value):
    high = value.astype(BF16)
    return high, (value - high.astype(F32)).astype(BF16)


def fold_rows(value, op):
    rows = value.shape[0]
    while rows > 8:
        rows //= 2
        value = op(value[:rows], value[rows:])
    return value


def to_row(ref, groups):
    return jnp.concatenate([ref[r : r + 1, :] for r in range(groups)], axis=1)


def from_row(ref, value, groups):
    for r in range(groups):
        ref[r : r + 1, :] = value[:, r * 128 : (r + 1) * 128]


def kernel(
    x_hbm, y_hbm, a_hbm, b_hbm,
    fg_hbm, smap_hbm, tmap_hbm,
    x_ref, y_ref, a_ref, b_ref, fg_ref, smap_ref, tmap_ref,
    xt, yk, t, ehi, elo, fb, part,
    f1_out, f1_in, f2_out, f2_in, g1_out, g1a_in, g1b_in, g2_out, g2y_in, g2_mid, g2x_in,
    sa_out, sa_in, sb_out, sb_in, row,
    tn, ax_in, ra, ay_in, by_in, rb, bx_in, fin_t,
    sn, sc_in, zs, z_in, fin, fin_in,
    send, recv, near,
):
    rows_at, cols_at = lax.axis_index("rows"), lax.axis_index("cols")
    my, mx = rows_at // NX, lax.rem(rows_at, NX)
    mz, mc = cols_at // NC, lax.rem(cols_at, NC)

    def xy(dy, dx):
        return (lax.rem(my + dy, NY) * NX + lax.rem(mx + dx, NX), cols_at)

    def zc(dz, dc):
        return (rows_at, lax.rem(mz + dz, NZ) * NC + lax.rem(mc + dc, NC))

    def push(src, dst, phase, device):
        pltpu.make_async_remote_copy(
            src_ref=src, dst_ref=dst, send_sem=send.at[phase], recv_sem=recv.at[phase],
            device_id=device, device_id_type=MESH,
        ).start()

    def await_bytes(ref, sem):
        pltpu.make_async_copy(ref, ref, sem).wait()

    def push_xy(src, slots, phase):
        for dy, dx in XY_OFFSETS:
            push(src, slots.at[dy * NX + dx], phase, xy(dy, dx))

    def push_zc(src, slots, phase):
        for dz, dc in ZC_OFFSETS:
            push(src, slots.at[dz * NC + dc], phase, zc(dz, dc))

    def fetch(src, dst, k):
        copy = pltpu.make_async_copy(src, dst, near.at[k])
        copy.start()
        return copy

    loads = [
        fetch(x_hbm, x_ref, 0),
        fetch(y_hbm, y_ref, 1),
        fetch(a_hbm, a_ref, 2),
        fetch(b_hbm, b_ref, 3),
    ]
    barrier = pltpu.get_barrier_semaphore()
    for dy, dx in XY_OFFSETS:
        pl.semaphore_signal(barrier, inc=1, device_id=xy(dy, dx), device_id_type=MESH)
    for dz, dc in ZC_OFFSETS:
        pl.semaphore_signal(barrier, inc=1, device_id=zc(dz, dc), device_id_type=MESH)

    loads[0].wait()
    x = x_ref[...]
    xs = x * (4.0 * LOG2E)
    xh, xm, xl = split3(xs)
    xt[:, 0:128] = jnp.concatenate([xh.astype(F32), xm.astype(F32)], axis=0).T.astype(BF16)
    xt[:, 128:256] = xt[:, 0:128]
    xt[:, 256:384] = jnp.concatenate([xh.astype(F32), xl.astype(F32)], axis=0).T.astype(BF16)
    xt[:, 384:512] = jnp.where(lax.broadcasted_iota(jnp.int32, (SRC, 128), 1) < 3, 1.0, 0.0).astype(BF16)
    loads[1].wait()
    y = y_ref[...]
    yh, ym, yl = split3(y)
    yk[0:64, :] = yh
    yk[64:128, :] = yh
    yk[128:192, :] = ym
    yk[192:256, :] = ym
    yk[256:320, :] = yl
    yk[320:384, :] = yh
    ny = jnp.sum(y * y, axis=0, keepdims=True) * (-2.0 * LOG2E)
    nh, nm, nl = split3(ny)
    pick = lax.broadcasted_iota(jnp.int32, (16, TGT), 0)
    norms = jnp.where(
        pick == 0, nh.astype(F32), jnp.where(pick == 1, nm.astype(F32), jnp.where(pick == 2, nl.astype(F32), 0.0))
    )
    yk[384:400, :] = norms.astype(BF16)
    yk[400:512, :] = jnp.zeros((112, TGT), BF16)

    def score(k):
        at = slice(k * 128, (k + 1) * 128)
        t[at, :] = jnp.dot(xt[at, :], yk[...], preferred_element_type=F32)

    def row_logs(k):
        at = slice(k * 128, (k + 1) * 128)
        highest = t[at, 0:128]
        for g in range(1, GROUPS):
            highest = jnp.maximum(highest, t[at, g * 128 : (g + 1) * 128])
        total = jnp.exp2(t[at, 0:128] - highest)
        for g in range(1, GROUPS):
            total += jnp.exp2(t[at, g * 128 : (g + 1) * 128] - highest)
        highest, total = highest.T, total.T
        top = jnp.max(highest, axis=0, keepdims=True)
        summed = jnp.sum(total * jnp.exp2(highest - top), axis=0, keepdims=True)
        f1_out[k : k + 1, :] = top + jnp.log(summed) * LOG2E

    score(0)
    for k in range(8):
        if k < 7:
            score(k + 1)
        row_logs(k)
    loads[2].wait()
    loads[3].wait()
    sa_out[...] = jnp.broadcast_to(jnp.sum(a_ref[...], axis=(0, 1), keepdims=True), (1, 128))
    sb_out[...] = jnp.broadcast_to(jnp.sum(b_ref[...], axis=(0, 1), keepdims=True), (1, 128))

    pl.semaphore_wait(barrier, len(XY_OFFSETS) + len(ZC_OFFSETS))
    push_zc(f1_out, f1_in, 0)
    push_xy(sa_out, sa_in, 1)
    push_zc(sb_out, sb_in, 2)

    f1_in[0] = f1_out[...]
    await_bytes(f1_in.at[pl.ds(1, 15)], recv.at[0])
    highest = jnp.max(f1_in[...], axis=0)
    summed = jnp.sum(jnp.exp2(f1_in[...] - highest[None]), axis=0)
    log_a = jnp.log(a_ref[...]) * LOG2E
    first_f = log_a - (highest + jnp.log(summed) * LOG2E)
    row[0:8, :] = first_f
    for r in range(8):
        fb[r * 128 : (r + 1) * 128, :] = jnp.broadcast_to(row[r : r + 1, :], (128, 128)).T

    WIDE = 512
    for c in range(TGT // WIDE):
        cs = slice(c * WIDE, (c + 1) * WIDE)

        def shifted(k, top):
            at = pl.ds(pl.multiple_of(k * 64, 64), 64)
            f = fb[at, :]
            value = t[at, cs] + jnp.concatenate([f] * (WIDE // 128), axis=1)
            t[at, cs] = value
            return jnp.maximum(top, fold_rows(value, jnp.maximum))

        top = lax.fori_loop(0, 16, shifted, jnp.full((8, WIDE), NEG, F32), unroll=2)
        top = jnp.max(top, axis=0, keepdims=True)

        def powers(k, total):
            at = pl.ds(pl.multiple_of(k * 64, 64), 64)
            e = jnp.exp2(t[at, cs] - top)
            t[at, cs] = e
            high, low = split2(e)
            ehi[at, cs] = high
            elo[at, cs] = low
            return total + fold_rows(e, jnp.add)

        total = lax.fori_loop(0, 16, powers, jnp.zeros((8, WIDE), F32), unroll=2)
        total = jnp.sum(total, axis=0, keepdims=True)
        logs = top + jnp.log(total) * LOG2E
        for r in range(WIDE // 128):
            at = c * (WIDE // 128) + r
            g1_out[at : at + 1, :] = logs[:, r * 128 : (r + 1) * 128]
            row[8 + at : 9 + at, :] = top[:, r * 128 : (r + 1) * 128]
        if c == 1:
            push_xy(g1_out.at[0:8], g1a_in, 3)
    push_xy(g1_out.at[8:16], g1b_in, 4)
    b = b_ref[...]
    log_b = jnp.log(b) * LOG2E

    def log_sum(slots):
        highest = jnp.max(slots[...], axis=0)
        return highest + jnp.log(jnp.sum(jnp.exp2(slots[...] - highest[None]), axis=0)) * LOG2E

    g1a_in[0] = g1_out[0:8, :]
    await_bytes(g1a_in.at[pl.ds(1, 31)], recv.at[3])
    low_logs = log_sum(g1a_in)
    g1b_in[0] = g1_out[8:16, :]
    await_bytes(g1b_in.at[pl.ds(1, 31)], recv.at[4])
    first_g = log_b - jnp.concatenate([low_logs, log_sum(g1b_in)], axis=0)
    row[8:24, :] = jnp.exp2(row[8:24, :] + first_g)
    scale = to_row(row.at[8:24, :], 16)

    def weighted(k, _):
        at = pl.ds(pl.multiple_of(k * 64, 64), 64)
        total = t[at, 0:128] * scale[:, 0:128]
        for g in range(1, GROUPS):
            gs = slice(g * 128, (g + 1) * 128)
            total += t[at, gs] * scale[:, gs]
        part[at, :] = total
        return 0

    lax.fori_loop(0, 16, weighted, 0, unroll=2)
    for r in range(8):
        f2_out[r : r + 1, :] = jnp.sum(part[r * 128 : (r + 1) * 128, :].T, axis=0, keepdims=True)
    push_zc(f2_out, f2_in, 5)
    f2_in[0] = f2_out[...]
    nx = jnp.sum(x * x, axis=0, keepdims=True) * (2.0 * LOG2E)
    from_row(row.at[24:32, :], nx, 8)
    await_bytes(f2_in.at[pl.ds(1, 15)], recv.at[5])
    sums = jnp.sum(f2_in[...], axis=0)
    ratio = a_ref[...] / sums
    row[32:40, :] = ratio
    u = to_row(row.at[32:40, :], 8)

    def stacked(points, weights):
        high, low = split2(points * weights)
        wh, wl = split2(weights)
        tail = lax.broadcasted_iota(jnp.int32, (16, weights.shape[1]), 0)
        pair = jnp.where(tail == 0, wh.astype(F32), jnp.where(tail == 1, wl.astype(F32), 0.0))
        return jnp.concatenate([high, low, pair.astype(BF16)], axis=0)

    def rows_of(dy):
        return pl.ds(pl.multiple_of(lax.rem(my + dy, NY) * 8, 8), 8)

    def cols_of(dx):
        return pl.ds(pl.multiple_of(lax.rem(mx + dx, NX) * 128, 128), 128)

    own_rows, own_cols = rows_of(0), cols_of(0)

    def gather_x(p):
        for dx in X_OFFSETS:
            push(tn.at[p, :, cols_of(dx)], ax_in.at[p, dx], 23 + p, xy(0, dx))

    def scatter_y(p):
        await_bytes(ax_in.at[p, pl.ds(1, 3)], recv.at[23 + p])
        ra[p] = tn[p, :, own_cols] + ax_in[p, 1] + ax_in[p, 2] + ax_in[p, 3]
        for dy in Y_OFFSETS:
            push(ra.at[p, rows_of(dy), :], ay_in.at[p, dy], 26 + p, xy(dy, 0))

    def return_y(p):
        await_bytes(ay_in.at[p, pl.ds(1, 7)], recv.at[26 + p])
        total = ra[p, own_rows, :]
        for k in range(1, NY):
            total += ay_in[p, k]
        fin_t[p] = total / row[pl.ds(56 + mx * 4 + p, 1), :]
        for dy in Y_OFFSETS:
            push(fin_t.at[p], tmap_ref.at[p, own_rows, own_cols], 29 + p, xy(dy, 0))
        tmap_ref[p, own_rows, own_cols] = fin_t[p]

    def return_x(p):
        await_bytes(ay_in.at[p, pl.ds(1, 7)], recv.at[29 + p])
        for dx in X_OFFSETS:
            push(tmap_ref.at[p, :, own_cols], tmap_ref.at[p, :, own_cols], 32 + p, xy(0, dx))

    xu = stacked(x, u)
    for half in range(2):
        for q in range(NX):
            cs = slice(q * 512 + half * 256, q * 512 + half * 256 + 256)
            one = jnp.dot(xu, ehi[:, cs], preferred_element_type=F32)
            two = jnp.dot(xu, elo[:, cs], preferred_element_type=F32)
            w = scale[:, cs]
            sums = (one[0:64] + one[64:128] + two[0:64]) * w
            tn[half * 2, :, q * 128 : (q + 1) * 128] = sums[:, 0:128]
            tn[half * 2 + 1, :, q * 128 : (q + 1) * 128] = sums[:, 128:256]
            mass = (one[128:129] + one[129:130] + two[128:129]) * w
            at = q * 4 + half * 2
            g2_out[at : at + 1, :] = mass[:, 0:128]
            g2_out[at + 1 : at + 2, :] = mass[:, 128:256]
        if half == 0:
            gather_x(0)
            gather_x(1)
    for dy in Y_OFFSETS:
        push(g2_out, g2y_in.at[dy], 6, xy(dy, 0))
    for dy in Y_OFFSETS:
        push(tn.at[3, rows_of(dy), :], by_in.at[dy], 9, xy(dy, 0))
    gather_x(2)

    scatter_y(0)
    scatter_y(1)
    g2y_in[0] = g2_out[...]
    await_bytes(g2y_in.at[pl.ds(1, 7)], recv.at[6])
    g2_mid[...] = jnp.sum(g2y_in[...], axis=0)
    for dx in X_OFFSETS:
        push(g2_mid, g2x_in.at[dx], 8, xy(0, dx))
    scatter_y(2)
    await_bytes(by_in.at[pl.ds(1, 7)], recv.at[9])
    total = tn[3, own_rows, :]
    for k in range(1, NY):
        total += by_in[k]
    rb[...] = total
    for dx in X_OFFSETS:
        push(rb.at[:, cols_of(dx)], bx_in.at[dx], 11, xy(0, dx))

    g2x_in[0] = g2_mid[...]
    await_bytes(g2x_in.at[pl.ds(1, 3)], recv.at[8])
    row[56:72, :] = jnp.sum(g2x_in[...], axis=0)
    ratio_g = b / row[56:72, :]
    row[72:88, :] = row[8:24, :] * ratio_g
    weights = to_row(row.at[72:88, :], 16)

    yq = stacked(y, weights)
    nt = (((1,), (1,)), ((), ()))
    partner = zc(0, 1)
    own_pair = mz // 2
    pairs = [lax.rem(own_pair + k, NZ // 2) for k in (2, 1, 3, 0)]

    def chunk(k):
        rs = pl.ds(pl.multiple_of(pairs[k] * 256, 256), 256)
        one = lax.dot_general(yq, ehi[rs, :], nt, preferred_element_type=F32)
        two = lax.dot_general(yq, elo[rs, :], nt, preferred_element_type=F32)
        sn[k, 0:64, :] = one[0:64] + one[64:128] + two[0:64]
        weight = one[128:129] + one[129:130] + two[128:129]
        sn[k, 64:72, :] = jnp.broadcast_to(weight, (8, 256))
        theirs = pl.ds(pl.multiple_of((1 - mc) * 32, 32), 32)
        push(sn.at[k, theirs], sc_in.at[k, pl.ds(0, 32)], 19 + k, partner)
        push(sn.at[k, pl.ds(64, 8)], sc_in.at[k, pl.ds(32, 8)], 19 + k, partner)

    def onward(k):
        await_bytes(sc_in.at[k], recv.at[19 + k])
        mine = pl.ds(pl.multiple_of(mc * 32, 32), 32)
        for e in range(2):
            es = slice(e * 128, (e + 1) * 128)
            zs[k * 2 + e, 0:32, :] = sn[k, mine, es] + sc_in[k, 0:32, es]
            zs[k * 2 + e, 32:40, :] = sn[k, 64:72, es] + sc_in[k, 32:40, es]
        if k < 3:
            for e in range(2):
                to = pairs[k] * 2 + e
                hops = lax.rem(to - mz + NZ, NZ)
                push(zs.at[k * 2 + e], z_in.at[hops], 15, (rows_at, to * NC + mc))
        else:
            to = own_pair * 2 + 1 - lax.rem(mz, 2)
            hops = lax.rem(to - mz + NZ, NZ)
            push(zs.at[6 + 1 - lax.rem(mz, 2)], z_in.at[hops], 15, (rows_at, to * NC + mc))

    chunk(0)
    return_y(0)
    return_y(1)
    await_bytes(bx_in.at[pl.ds(1, 3)], recv.at[11])
    fin_t[3] = (rb[:, own_cols] + bx_in[1] + bx_in[2] + bx_in[3]) / row[pl.ds(56 + mx * 4 + 3, 1), :]
    for dx in X_OFFSETS:
        push(fin_t.at[3], tmap_ref.at[3, own_rows, own_cols], 14, xy(0, dx))
    tmap_ref[3, own_rows, own_cols] = fin_t[3]
    chunk(1)
    onward(0)
    return_y(2)
    chunk(2)
    onward(1)
    chunk(3)
    onward(2)
    onward(3)

    return_x(0)
    await_bytes(bx_in.at[pl.ds(1, 3)], recv.at[14])
    for dy in Y_OFFSETS:
        push(tmap_ref.at[3, own_rows, :], tmap_ref.at[3, own_rows, :], 16, xy(dy, 0))
    return_x(1)
    return_x(2)

    sa_in[0] = sa_out[...]
    sb_in[0] = sb_out[...]
    await_bytes(sa_in.at[pl.ds(1, 31)], recv.at[1])
    await_bytes(sb_in.at[pl.ds(1, 15)], recv.at[2])
    log_sa = jnp.log(jnp.sum(sa_in[...], axis=0))
    log_sb = jnp.log(jnp.sum(sb_in[...], axis=0))
    fg_ref[0:8, :] = (0.5 * LN2) * (first_f + row[24:32, :]) + 0.5 * jnp.log(ratio) - (log_sa - 0.5 * log_sb)
    fg_ref[8:24, :] = (0.5 * LN2) * first_g + 0.5 * jnp.log(ratio_g) - (log_sb - log_sa)
    stores = [fetch(fg_ref, fg_hbm, 4)]

    await_bytes(z_in.at[pl.ds(1, 7)], recv.at[15])
    total = zs[6 + lax.rem(mz, 2)]
    for k in range(1, NZ):
        total += z_in[k]
    fin[...] = total[0:32] / total[32:33]
    push(fin, fin_in, 18, partner)
    await_bytes(fin_in, recv.at[18])
    mine, other = fin[...], fin_in[...]
    low = jnp.where(mc == 0, mine, other)
    high = jnp.where(mc == 0, other, mine)
    both = jnp.concatenate([low, high], axis=0)
    smap_ref[...] = jnp.where(mc == 0, both[:, 0:64], both[:, 64:128])
    stores.append(fetch(smap_ref, smap_hbm, 5))

    def store(p):
        for q in range(NX):
            place = tmap_hbm.at[:, q * 512 + p * 128 : q * 512 + p * 128 + 128]
            stores.append(fetch(tmap_ref.at[p, :, q * 128 : q * 128 + 128], place, 6 + p * 4 + q))

    await_bytes(ax_in.at[0, pl.ds(1, 3)], recv.at[32])
    store(0)
    await_bytes(ax_in.at[1, pl.ds(1, 3)], recv.at[33])
    store(1)
    await_bytes(by_in.at[pl.ds(1, 7)], recv.at[16])
    store(3)
    await_bytes(ax_in.at[2, pl.ds(1, 3)], recv.at[34])
    store(2)

    await_bytes(f1_in.at[pl.ds(1, 15)], send.at[0])
    await_bytes(sa_in.at[pl.ds(1, 31)], send.at[1])
    await_bytes(sb_in.at[pl.ds(1, 15)], send.at[2])
    await_bytes(g1a_in.at[pl.ds(1, 31)], send.at[3])
    await_bytes(g1b_in.at[pl.ds(1, 31)], send.at[4])
    await_bytes(f2_in.at[pl.ds(1, 15)], send.at[5])
    await_bytes(g2y_in.at[pl.ds(1, 7)], send.at[6])
    await_bytes(g2x_in.at[pl.ds(1, 3)], send.at[8])
    await_bytes(by_in.at[pl.ds(1, 7)], send.at[9])
    await_bytes(bx_in.at[pl.ds(1, 3)], send.at[11])
    for k in range(4):
        await_bytes(sc_in.at[k], send.at[19 + k])
    await_bytes(bx_in.at[pl.ds(1, 3)], send.at[14])
    await_bytes(z_in.at[pl.ds(1, 7)], send.at[15])
    await_bytes(by_in.at[pl.ds(1, 7)], send.at[16])
    for p in range(3):
        await_bytes(ax_in.at[p, pl.ds(1, 3)], send.at[23 + p])
        await_bytes(ay_in.at[p, pl.ds(1, 7)], send.at[26 + p])
        await_bytes(ay_in.at[p, pl.ds(1, 7)], send.at[29 + p])
        await_bytes(ax_in.at[p, pl.ds(1, 3)], send.at[32 + p])
    await_bytes(fin_in, send.at[18])
    for copy in stores:
        copy.wait()


def finish(fg, sm, tm, f_hbm, g_hbm, smap_hbm, tmap_hbm, fg_v, sm_v, tm_v, come, go):
    loads = [pltpu.make_async_copy(tm.at[k * 32 : k * 32 + 32], tm_v.at[k * 32 : k * 32 + 32], come.at[k]) for k in range(2)]
    loads += [pltpu.make_async_copy(sm, sm_v, come.at[2]), pltpu.make_async_copy(fg, fg_v, come.at[3])]
    stores = [pltpu.make_async_copy(tm_v.at[k * 32 : k * 32 + 32], tmap_hbm.at[k * 32 : k * 32 + 32], go.at[k]) for k in range(2)]
    stores += [
        pltpu.make_async_copy(sm_v, smap_hbm, go.at[2]),
        pltpu.make_async_copy(fg_v.at[0:8], f_hbm, go.at[3]),
        pltpu.make_async_copy(fg_v.at[8:24], g_hbm, go.at[4]),
    ]
    for copy in loads:
        copy.start()
    for k, copy in enumerate(loads):
        copy.wait()
        stores[k].start()
    stores[4].start()
    for copy in stores:
        copy.wait()


def local(source_cells, target_cells, source_mass, target_mass):
    anywhere = pl.BlockSpec(memory_space=pl.ANY)
    results = pl.pallas_call(
        kernel,
        out_shape=(
            jax.ShapeDtypeStruct((24, 128), F32),
            jax.ShapeDtypeStruct((DIMS, 64), F32),
            jax.ShapeDtypeStruct((DIMS, TGT), F32),
        ),
        in_specs=[anywhere] * 4,
        out_specs=(anywhere,) * 3,
        scratch_shapes=[
            pltpu.VMEM((DIMS, SRC), F32),
            pltpu.VMEM((DIMS, TGT), F32),
            pltpu.VMEM((8, 128), F32),
            pltpu.VMEM((16, 128), F32),
            pltpu.VMEM((24, 128), F32),
            pltpu.VMEM((DIMS, 64), F32),
            pltpu.VMEM((4, DIMS, 512), F32),
            pltpu.VMEM((SRC, 512), BF16),
            pltpu.VMEM((512, TGT), BF16),
            pltpu.VMEM((SRC, TGT), F32),
            pltpu.VMEM((SRC, TGT), BF16),
            pltpu.VMEM((SRC, TGT), BF16),
            pltpu.VMEM((SRC, 128), F32),
            pltpu.VMEM((SRC, 128), F32),
            pltpu.VMEM((8, 128), F32),
            pltpu.VMEM((16, 8, 128), F32),
            pltpu.VMEM((8, 128), F32),
            pltpu.VMEM((16, 8, 128), F32),
            pltpu.VMEM((16, 128), F32),
            pltpu.VMEM((32, 8, 128), F32),
            pltpu.VMEM((32, 8, 128), F32),
            pltpu.VMEM((16, 128), F32),
            pltpu.VMEM((NY, 16, 128), F32),
            pltpu.VMEM((16, 128), F32),
            pltpu.VMEM((NX, 16, 128), F32),
            pltpu.VMEM((1, 128), F32),
            pltpu.VMEM((32, 1, 128), F32),
            pltpu.VMEM((1, 128), F32),
            pltpu.VMEM((16, 1, 128), F32),
            pltpu.VMEM((88, 128), F32),
            pltpu.VMEM((4, DIMS, 512), F32),
            pltpu.VMEM((3, NX, DIMS, 128), F32),
            pltpu.VMEM((3, DIMS, 128), F32),
            pltpu.VMEM((3, NY, 8, 128), F32),
            pltpu.VMEM((NY, 8, 512), F32),
            pltpu.VMEM((8, 512), F32),
            pltpu.VMEM((NX, 8, 128), F32),
            pltpu.VMEM((4, 8, 128), F32),
            pltpu.VMEM((4, 72, 256), F32),
            pltpu.VMEM((4, 40, 256), F32),
            pltpu.VMEM((NZ, 40, 128), F32),
            pltpu.VMEM((NZ, 40, 128), F32),
            pltpu.VMEM((32, 128), F32),
            pltpu.VMEM((32, 128), F32),
            pltpu.SemaphoreType.DMA((35,)),
            pltpu.SemaphoreType.DMA((35,)),
            pltpu.SemaphoreType.DMA((22,)),
        ],
        compiler_params=pltpu.CompilerParams(
            collective_id=0, has_side_effects=True, vmem_limit_bytes=60 << 20
        ),
    )(source_cells, target_cells, source_mass.reshape(8, 128), target_mass.reshape(16, 128))
    f, g, smap, tmap = pl.pallas_call(
        finish,
        out_shape=(
            jax.ShapeDtypeStruct((8, 128), F32),
            jax.ShapeDtypeStruct((16, 128), F32),
            jax.ShapeDtypeStruct((DIMS, 64), F32),
            jax.ShapeDtypeStruct((DIMS, TGT), F32),
        ),
        in_specs=[anywhere] * 3,
        out_specs=(anywhere,) * 4,
        scratch_shapes=[
            pltpu.VMEM((24, 128), F32),
            pltpu.VMEM((DIMS, 64), F32),
            pltpu.VMEM((DIMS, TGT), F32),
            pltpu.SemaphoreType.DMA((4,)),
            pltpu.SemaphoreType.DMA((5,)),
        ],
    )(*results)
    return f.reshape(-1), g.reshape(-1), smap, tmap


def solution(mesh):
    in_specs = (P(None, "rows"), P(None, "cols"), P("rows"), P("cols"))
    out_specs = (P("rows"), P("cols"), P(None, ("rows", "cols")), P(None, "cols"))
    return jax.shard_map(local, mesh=mesh, in_specs=in_specs, out_specs=out_specs, check_vma=False)
```

```python
import functools
import math

import jax
import jax.numpy as jnp
from jax import lax
from jax.experimental import pallas as pl
from jax.experimental.pallas import tpu as pltpu
from jax.sharding import PartitionSpec as P

MESH = pl.DeviceIdType.MESH
F32 = jnp.float32
BF16 = jnp.bfloat16
LOG2E = math.log2(math.e)
LN2 = math.log(2.0)
NEG = -3.0e38

DIMS = 64
SRC = 1024
TGT = 2048
NX, NY, NZ, NC = 4, 8, 8, 2
GROUPS = 16


def far(n, r):
    return min(r, n - r)


XY_OFFSETS = sorted(
    [(dy, dx) for dy in range(NY) for dx in range(NX) if dy or dx],
    key=lambda o: -(far(NY, o[0]) + far(NX, o[1])),
)
ZC_OFFSETS = sorted(
    [(dz, dc) for dz in range(NZ) for dc in range(NC) if dz or dc],
    key=lambda o: -(far(NZ, o[0]) + 0.3 * o[1]),
)
Y_OFFSETS = sorted(range(1, NY), key=lambda r: -far(NY, r))
X_OFFSETS = sorted(range(1, NX), key=lambda r: -far(NX, r))
Z_OFFSETS = sorted(range(1, NZ), key=lambda r: -far(NZ, r))


def split3(value):
    high = value.astype(BF16)
    rest = value - high.astype(F32)
    middle = rest.astype(BF16)
    low = (rest - middle.astype(F32)).astype(BF16)
    return high, middle, low


def split2(value):
    high = value.astype(BF16)
    return high, (value - high.astype(F32)).astype(BF16)


def fold_rows(value, op):
    rows = value.shape[0]
    while rows > 8:
        rows //= 2
        value = op(value[:rows], value[rows:])
    return value


def to_row(ref, groups):
    return jnp.concatenate([ref[r : r + 1, :] for r in range(groups)], axis=1)


def from_row(ref, value, groups):
    for r in range(groups):
        ref[r : r + 1, :] = value[:, r * 128 : (r + 1) * 128]


def kernel(
    x_hbm, y_hbm, a_hbm, b_hbm,
    fg_hbm, smap_hbm, tmap_hbm,
    x_ref, y_ref, a_ref, b_ref, fg_ref, smap_ref, tmap_ref,
    xt, yk, t, ehi, elo, fb, part,
    f1_out, f1_in, f2_out, f2_in, g1_out, g1a_in, g1b_in, g2_out, g2y_in, g2_mid, g2x_in,
    sa_out, sa_in, sb_out, sb_in, row,
    tn, ax_in, ra, ay_in, by_in, rb, bx_in, fin_t,
    sn, sc_in, zs, z_in, fin, fin_in,
    send, recv, near,
):
    rows_at, cols_at = lax.axis_index("rows"), lax.axis_index("cols")
    my, mx = rows_at // NX, lax.rem(rows_at, NX)
    mz, mc = cols_at // NC, lax.rem(cols_at, NC)

    def xy(dy, dx):
        return (lax.rem(my + dy, NY) * NX + lax.rem(mx + dx, NX), cols_at)

    def zc(dz, dc):
        return (rows_at, lax.rem(mz + dz, NZ) * NC + lax.rem(mc + dc, NC))

    def push(src, dst, phase, device):
        pltpu.make_async_remote_copy(
            src_ref=src, dst_ref=dst, send_sem=send.at[phase], recv_sem=recv.at[phase],
            device_id=device, device_id_type=MESH,
        ).start()

    def await_bytes(ref, sem):
        pltpu.make_async_copy(ref, ref, sem).wait()

    def push_xy(src, slots, phase):
        for dy, dx in XY_OFFSETS:
            push(src, slots.at[dy * NX + dx], phase, xy(dy, dx))

    def push_zc(src, slots, phase):
        for dz, dc in ZC_OFFSETS:
            push(src, slots.at[dz * NC + dc], phase, zc(dz, dc))

    def fetch(src, dst, k):
        copy = pltpu.make_async_copy(src, dst, near.at[k])
        copy.start()
        return copy

    loads = [
        fetch(x_hbm, x_ref, 0),
        fetch(y_hbm, y_ref, 1),
        fetch(a_hbm, a_ref, 2),
        fetch(b_hbm, b_ref, 3),
    ]
    barrier = pltpu.get_barrier_semaphore()
    for dy, dx in XY_OFFSETS:
        pl.semaphore_signal(barrier, inc=1, device_id=xy(dy, dx), device_id_type=MESH)
    for dz, dc in ZC_OFFSETS:
        pl.semaphore_signal(barrier, inc=1, device_id=zc(dz, dc), device_id_type=MESH)

    loads[0].wait()
    x = x_ref[...]
    xs = x * (4.0 * LOG2E)
    xh, xm, xl = split3(xs)
    xt[:, 0:128] = jnp.concatenate([xh.astype(F32), xm.astype(F32)], axis=0).T.astype(BF16)
    xt[:, 128:256] = xt[:, 0:128]
    xt[:, 256:384] = jnp.concatenate([xh.astype(F32), xl.astype(F32)], axis=0).T.astype(BF16)
    xt[:, 384:512] = jnp.where(lax.broadcasted_iota(jnp.int32, (SRC, 128), 1) < 3, 1.0, 0.0).astype(BF16)
    loads[1].wait()
    y = y_ref[...]
    yh, ym, yl = split3(y)
    yk[0:64, :] = yh
    yk[64:128, :] = yh
    yk[128:192, :] = ym
    yk[192:256, :] = ym
    yk[256:320, :] = yl
    yk[320:384, :] = yh
    ny = jnp.sum(y * y, axis=0, keepdims=True) * (-2.0 * LOG2E)
    nh, nm, nl = split3(ny)
    pick = lax.broadcasted_iota(jnp.int32, (16, TGT), 0)
    norms = jnp.where(
        pick == 0, nh.astype(F32), jnp.where(pick == 1, nm.astype(F32), jnp.where(pick == 2, nl.astype(F32), 0.0))
    )
    yk[384:400, :] = norms.astype(BF16)
    yk[400:512, :] = jnp.zeros((112, TGT), BF16)

    def score(k):
        at = slice(k * 128, (k + 1) * 128)
        t[at, :] = jnp.dot(xt[at, :], yk[...], preferred_element_type=F32)

    def row_logs(k):
        at = slice(k * 128, (k + 1) * 128)
        highest = t[at, 0:128]
        for g in range(1, GROUPS):
            highest = jnp.maximum(highest, t[at, g * 128 : (g + 1) * 128])
        total = jnp.exp2(t[at, 0:128] - highest)
        for g in range(1, GROUPS):
            total += jnp.exp2(t[at, g * 128 : (g + 1) * 128] - highest)
        highest, total = highest.T, total.T
        top = jnp.max(highest, axis=0, keepdims=True)
        summed = jnp.sum(total * jnp.exp2(highest - top), axis=0, keepdims=True)
        f1_out[k : k + 1, :] = top + jnp.log(summed) * LOG2E

    score(0)
    for k in range(8):
        if k < 7:
            score(k + 1)
        row_logs(k)
    loads[2].wait()
    loads[3].wait()
    sa_out[...] = jnp.broadcast_to(jnp.sum(a_ref[...], axis=(0, 1), keepdims=True), (1, 128))
    sb_out[...] = jnp.broadcast_to(jnp.sum(b_ref[...], axis=(0, 1), keepdims=True), (1, 128))

    pl.semaphore_wait(barrier, len(XY_OFFSETS) + len(ZC_OFFSETS))
    push_zc(f1_out, f1_in, 0)
    push_xy(sa_out, sa_in, 1)
    push_zc(sb_out, sb_in, 2)

    f1_in[0] = f1_out[...]
    await_bytes(f1_in.at[pl.ds(1, 15)], recv.at[0])
    highest = jnp.max(f1_in[...], axis=0)
    summed = jnp.sum(jnp.exp2(f1_in[...] - highest[None]), axis=0)
    log_a = jnp.log(a_ref[...]) * LOG2E
    first_f = log_a - (highest + jnp.log(summed) * LOG2E)
    row[0:8, :] = first_f
    for r in range(8):
        fb[r * 128 : (r + 1) * 128, :] = jnp.broadcast_to(row[r : r + 1, :], (128, 128)).T

    WIDE = 512
    for c in range(TGT // WIDE):
        cs = slice(c * WIDE, (c + 1) * WIDE)

        def shifted(k, top):
            at = pl.ds(pl.multiple_of(k * 64, 64), 64)
            f = fb[at, :]
            value = t[at, cs] + jnp.concatenate([f] * (WIDE // 128), axis=1)
            t[at, cs] = value
            return jnp.maximum(top, fold_rows(value, jnp.maximum))

        top = lax.fori_loop(0, 16, shifted, jnp.full((8, WIDE), NEG, F32), unroll=2)
        top = jnp.max(top, axis=0, keepdims=True)

        def powers(k, total):
            at = pl.ds(pl.multiple_of(k * 64, 64), 64)
            e = jnp.exp2(t[at, cs] - top)
            t[at, cs] = e
            high, low = split2(e)
            ehi[at, cs] = high
            elo[at, cs] = low
            return total + fold_rows(e, jnp.add)

        total = lax.fori_loop(0, 16, powers, jnp.zeros((8, WIDE), F32), unroll=2)
        total = jnp.sum(total, axis=0, keepdims=True)
        logs = top + jnp.log(total) * LOG2E
        for r in range(WIDE // 128):
            at = c * (WIDE // 128) + r
            g1_out[at : at + 1, :] = logs[:, r * 128 : (r + 1) * 128]
            row[8 + at : 9 + at, :] = top[:, r * 128 : (r + 1) * 128]
        if c == 1:
            push_xy(g1_out.at[0:8], g1a_in, 3)
    push_xy(g1_out.at[8:16], g1b_in, 4)
    b = b_ref[...]
    log_b = jnp.log(b) * LOG2E

    def log_sum(slots):
        highest = jnp.max(slots[...], axis=0)
        return highest + jnp.log(jnp.sum(jnp.exp2(slots[...] - highest[None]), axis=0)) * LOG2E

    g1a_in[0] = g1_out[0:8, :]
    await_bytes(g1a_in.at[pl.ds(1, 31)], recv.at[3])
    low_logs = log_sum(g1a_in)
    g1b_in[0] = g1_out[8:16, :]
    await_bytes(g1b_in.at[pl.ds(1, 31)], recv.at[4])
    first_g = log_b - jnp.concatenate([low_logs, log_sum(g1b_in)], axis=0)
    row[8:24, :] = jnp.exp2(row[8:24, :] + first_g)
    scale = to_row(row.at[8:24, :], 16)

    def weighted(k, _):
        at = pl.ds(pl.multiple_of(k * 64, 64), 64)
        total = t[at, 0:128] * scale[:, 0:128]
        for g in range(1, GROUPS):
            gs = slice(g * 128, (g + 1) * 128)
            total += t[at, gs] * scale[:, gs]
        part[at, :] = total
        return 0

    lax.fori_loop(0, 16, weighted, 0, unroll=2)
    for r in range(8):
        f2_out[r : r + 1, :] = jnp.sum(part[r * 128 : (r + 1) * 128, :].T, axis=0, keepdims=True)
    push_zc(f2_out, f2_in, 5)
    f2_in[0] = f2_out[...]
    nx = jnp.sum(x * x, axis=0, keepdims=True) * (2.0 * LOG2E)
    from_row(row.at[24:32, :], nx, 8)
    await_bytes(f2_in.at[pl.ds(1, 15)], recv.at[5])
    sums = jnp.sum(f2_in[...], axis=0)
    ratio = a_ref[...] / sums
    row[32:40, :] = ratio
    u = to_row(row.at[32:40, :], 8)

    def stacked(points, weights):
        high, low = split2(points * weights)
        wh, wl = split2(weights)
        tail = lax.broadcasted_iota(jnp.int32, (16, weights.shape[1]), 0)
        pair = jnp.where(tail == 0, wh.astype(F32), jnp.where(tail == 1, wl.astype(F32), 0.0))
        return jnp.concatenate([high, low, pair.astype(BF16)], axis=0)

    def rows_of(dy):
        return pl.ds(pl.multiple_of(lax.rem(my + dy, NY) * 8, 8), 8)

    def cols_of(dx):
        return pl.ds(pl.multiple_of(lax.rem(mx + dx, NX) * 128, 128), 128)

    own_rows, own_cols = rows_of(0), cols_of(0)

    def gather_x(p):
        for dx in X_OFFSETS:
            push(tn.at[p, :, cols_of(dx)], ax_in.at[p, dx], 23 + p, xy(0, dx))

    def scatter_y(p):
        await_bytes(ax_in.at[p, pl.ds(1, 3)], recv.at[23 + p])
        ra[p] = tn[p, :, own_cols] + ax_in[p, 1] + ax_in[p, 2] + ax_in[p, 3]
        for dy in Y_OFFSETS:
            push(ra.at[p, rows_of(dy), :], ay_in.at[p, dy], 26 + p, xy(dy, 0))

    def return_y(p):
        await_bytes(ay_in.at[p, pl.ds(1, 7)], recv.at[26 + p])
        total = ra[p, own_rows, :]
        for k in range(1, NY):
            total += ay_in[p, k]
        fin_t[p] = total / row[pl.ds(56 + mx * 4 + p, 1), :]
        for dy in Y_OFFSETS:
            push(fin_t.at[p], tmap_ref.at[p, own_rows, own_cols], 29 + p, xy(dy, 0))
        tmap_ref[p, own_rows, own_cols] = fin_t[p]

    def return_x(p):
        await_bytes(ay_in.at[p, pl.ds(1, 7)], recv.at[29 + p])
        for dx in X_OFFSETS:
            push(tmap_ref.at[p, :, own_cols], tmap_ref.at[p, :, own_cols], 32 + p, xy(0, dx))

    xu = stacked(x, u)
    for half in range(2):
        for q in range(NX):
            cs = slice(q * 512 + half * 256, q * 512 + half * 256 + 256)
            one = jnp.dot(xu, ehi[:, cs], preferred_element_type=F32)
            two = jnp.dot(xu, elo[:, cs], preferred_element_type=F32)
            w = scale[:, cs]
            sums = (one[0:64] + one[64:128] + two[0:64]) * w
            tn[half * 2, :, q * 128 : (q + 1) * 128] = sums[:, 0:128]
            tn[half * 2 + 1, :, q * 128 : (q + 1) * 128] = sums[:, 128:256]
            mass = (one[128:129] + one[129:130] + two[128:129]) * w
            at = q * 4 + half * 2
            g2_out[at : at + 1, :] = mass[:, 0:128]
            g2_out[at + 1 : at + 2, :] = mass[:, 128:256]
        if half == 0:
            gather_x(0)
            gather_x(1)
    for dy in Y_OFFSETS:
        push(g2_out, g2y_in.at[dy], 6, xy(dy, 0))
    for dy in Y_OFFSETS:
        push(tn.at[3, rows_of(dy), :], by_in.at[dy], 9, xy(dy, 0))
    gather_x(2)

    scatter_y(0)
    scatter_y(1)
    g2y_in[0] = g2_out[...]
    await_bytes(g2y_in.at[pl.ds(1, 7)], recv.at[6])
    g2_mid[...] = jnp.sum(g2y_in[...], axis=0)
    for dx in X_OFFSETS:
        push(g2_mid, g2x_in.at[dx], 8, xy(0, dx))
    scatter_y(2)
    await_bytes(by_in.at[pl.ds(1, 7)], recv.at[9])
    total = tn[3, own_rows, :]
    for k in range(1, NY):
        total += by_in[k]
    rb[...] = total
    for dx in X_OFFSETS:
        push(rb.at[:, cols_of(dx)], bx_in.at[dx], 11, xy(0, dx))

    g2x_in[0] = g2_mid[...]
    await_bytes(g2x_in.at[pl.ds(1, 3)], recv.at[8])
    row[56:72, :] = jnp.sum(g2x_in[...], axis=0)
    ratio_g = b / row[56:72, :]
    row[72:88, :] = row[8:24, :] * ratio_g
    weights = to_row(row.at[72:88, :], 16)

    yq = stacked(y, weights)
    nt = (((1,), (1,)), ((), ()))
    partner = zc(0, 1)
    own_pair = mz // 2
    pairs = [lax.rem(own_pair + k, NZ // 2) for k in (2, 1, 3, 0)]

    def chunk(k):
        rs = pl.ds(pl.multiple_of(pairs[k] * 256, 256), 256)
        one = lax.dot_general(yq, ehi[rs, :], nt, preferred_element_type=F32)
        two = lax.dot_general(yq, elo[rs, :], nt, preferred_element_type=F32)
        sn[k, 0:32, :] = one[0:32] + one[64:96] + two[0:32]
        sn[k, 40:72, :] = one[32:64] + one[96:128] + two[32:64]
        weight = jnp.broadcast_to(one[128:129] + one[129:130] + two[128:129], (8, 256))
        sn[k, 32:40, :] = weight
        sn[k, 72:80, :] = weight
        theirs = pl.ds(pl.multiple_of((1 - mc) * 40, 8), 40)
        push(sn.at[k, theirs], sc_in.at[k], 19 + k, partner)

    def onward(k):
        await_bytes(sc_in.at[k], recv.at[19 + k])
        mine = pl.ds(pl.multiple_of(mc * 40, 8), 40)
        for e in range(2):
            es = slice(e * 128, (e + 1) * 128)
            zs[k * 2 + e] = sn[k, mine, es] + sc_in[k, :, es]
        if k < 3:
            for e in range(2):
                to = pairs[k] * 2 + e
                hops = lax.rem(to - mz + NZ, NZ)
                push(zs.at[k * 2 + e], z_in.at[hops], 15, (rows_at, to * NC + mc))
        else:
            to = own_pair * 2 + 1 - lax.rem(mz, 2)
            hops = lax.rem(to - mz + NZ, NZ)
            push(zs.at[6 + 1 - lax.rem(mz, 2)], z_in.at[hops], 15, (rows_at, to * NC + mc))

    chunk(0)
    chunk(1)
    onward(0)
    return_y(0)
    return_y(1)
    chunk(2)
    onward(1)
    await_bytes(bx_in.at[pl.ds(1, 3)], recv.at[11])
    fin_t[3] = (rb[:, own_cols] + bx_in[1] + bx_in[2] + bx_in[3]) / row[pl.ds(56 + mx * 4 + 3, 1), :]
    for dx in X_OFFSETS:
        push(fin_t.at[3], tmap_ref.at[3, own_rows, own_cols], 14, xy(0, dx))
    tmap_ref[3, own_rows, own_cols] = fin_t[3]
    chunk(3)
    onward(2)
    return_y(2)
    onward(3)

    return_x(0)
    await_bytes(bx_in.at[pl.ds(1, 3)], recv.at[14])
    for dy in Y_OFFSETS:
        push(tmap_ref.at[3, own_rows, :], tmap_ref.at[3, own_rows, :], 16, xy(dy, 0))
    return_x(1)
    return_x(2)

    sa_in[0] = sa_out[...]
    sb_in[0] = sb_out[...]
    await_bytes(sa_in.at[pl.ds(1, 31)], recv.at[1])
    await_bytes(sb_in.at[pl.ds(1, 15)], recv.at[2])
    log_sa = jnp.log(jnp.sum(sa_in[...], axis=0))
    log_sb = jnp.log(jnp.sum(sb_in[...], axis=0))
    fg_ref[0:8, :] = (0.5 * LN2) * (first_f + row[24:32, :]) + 0.5 * jnp.log(ratio) - (log_sa - 0.5 * log_sb)
    fg_ref[8:24, :] = (0.5 * LN2) * first_g + 0.5 * jnp.log(ratio_g) - (log_sb - log_sa)
    stores = [fetch(fg_ref, fg_hbm, 4)]

    await_bytes(z_in.at[pl.ds(1, 7)], recv.at[15])
    total = zs[6 + lax.rem(mz, 2)]
    for k in range(1, NZ):
        total += z_in[k]
    fin[...] = total[0:32] / total[32:33]
    push(fin, fin_in, 18, partner)
    await_bytes(fin_in, recv.at[18])
    mine, other = fin[...], fin_in[...]
    low = jnp.where(mc == 0, mine, other)
    high = jnp.where(mc == 0, other, mine)
    both = jnp.concatenate([low, high], axis=0)
    smap_ref[...] = jnp.where(mc == 0, both[:, 0:64], both[:, 64:128])
    stores.append(fetch(smap_ref, smap_hbm, 5))

    def store(p):
        for q in range(NX):
            place = tmap_hbm.at[:, q * 512 + p * 128 : q * 512 + p * 128 + 128]
            stores.append(fetch(tmap_ref.at[p, :, q * 128 : q * 128 + 128], place, 6 + p * 4 + q))

    await_bytes(ax_in.at[0, pl.ds(1, 3)], recv.at[32])
    store(0)
    await_bytes(ax_in.at[1, pl.ds(1, 3)], recv.at[33])
    store(1)
    await_bytes(by_in.at[pl.ds(1, 7)], recv.at[16])
    store(3)
    await_bytes(ax_in.at[2, pl.ds(1, 3)], recv.at[34])
    store(2)

    await_bytes(f1_in.at[pl.ds(1, 15)], send.at[0])
    await_bytes(sa_in.at[pl.ds(1, 31)], send.at[1])
    await_bytes(sb_in.at[pl.ds(1, 15)], send.at[2])
    await_bytes(g1a_in.at[pl.ds(1, 31)], send.at[3])
    await_bytes(g1b_in.at[pl.ds(1, 31)], send.at[4])
    await_bytes(f2_in.at[pl.ds(1, 15)], send.at[5])
    await_bytes(g2y_in.at[pl.ds(1, 7)], send.at[6])
    await_bytes(g2x_in.at[pl.ds(1, 3)], send.at[8])
    await_bytes(by_in.at[pl.ds(1, 7)], send.at[9])
    await_bytes(bx_in.at[pl.ds(1, 3)], send.at[11])
    for k in range(4):
        await_bytes(sc_in.at[k], send.at[19 + k])
    await_bytes(bx_in.at[pl.ds(1, 3)], send.at[14])
    await_bytes(z_in.at[pl.ds(1, 7)], send.at[15])
    await_bytes(by_in.at[pl.ds(1, 7)], send.at[16])
    for p in range(3):
        await_bytes(ax_in.at[p, pl.ds(1, 3)], send.at[23 + p])
        await_bytes(ay_in.at[p, pl.ds(1, 7)], send.at[26 + p])
        await_bytes(ay_in.at[p, pl.ds(1, 7)], send.at[29 + p])
        await_bytes(ax_in.at[p, pl.ds(1, 3)], send.at[32 + p])
    await_bytes(fin_in, send.at[18])
    for copy in stores:
        copy.wait()


def finish(fg, sm, tm, f_hbm, g_hbm, smap_hbm, tmap_hbm, fg_v, sm_v, tm_v, come, go):
    loads = [pltpu.make_async_copy(tm.at[k * 32 : k * 32 + 32], tm_v.at[k * 32 : k * 32 + 32], come.at[k]) for k in range(2)]
    loads += [pltpu.make_async_copy(sm, sm_v, come.at[2]), pltpu.make_async_copy(fg, fg_v, come.at[3])]
    stores = [pltpu.make_async_copy(tm_v.at[k * 32 : k * 32 + 32], tmap_hbm.at[k * 32 : k * 32 + 32], go.at[k]) for k in range(2)]
    stores += [
        pltpu.make_async_copy(sm_v, smap_hbm, go.at[2]),
        pltpu.make_async_copy(fg_v.at[0:8], f_hbm, go.at[3]),
        pltpu.make_async_copy(fg_v.at[8:24], g_hbm, go.at[4]),
    ]
    for copy in loads:
        copy.start()
    for k, copy in enumerate(loads):
        copy.wait()
        stores[k].start()
    stores[4].start()
    for copy in stores:
        copy.wait()


def local(source_cells, target_cells, source_mass, target_mass):
    anywhere = pl.BlockSpec(memory_space=pl.ANY)
    results = pl.pallas_call(
        kernel,
        out_shape=(
            jax.ShapeDtypeStruct((24, 128), F32),
            jax.ShapeDtypeStruct((DIMS, 64), F32),
            jax.ShapeDtypeStruct((DIMS, TGT), F32),
        ),
        in_specs=[anywhere] * 4,
        out_specs=(anywhere,) * 3,
        scratch_shapes=[
            pltpu.VMEM((DIMS, SRC), F32),
            pltpu.VMEM((DIMS, TGT), F32),
            pltpu.VMEM((8, 128), F32),
            pltpu.VMEM((16, 128), F32),
            pltpu.VMEM((24, 128), F32),
            pltpu.VMEM((DIMS, 64), F32),
            pltpu.VMEM((4, DIMS, 512), F32),
            pltpu.VMEM((SRC, 512), BF16),
            pltpu.VMEM((512, TGT), BF16),
            pltpu.VMEM((SRC, TGT), F32),
            pltpu.VMEM((SRC, TGT), BF16),
            pltpu.VMEM((SRC, TGT), BF16),
            pltpu.VMEM((SRC, 128), F32),
            pltpu.VMEM((SRC, 128), F32),
            pltpu.VMEM((8, 128), F32),
            pltpu.VMEM((16, 8, 128), F32),
            pltpu.VMEM((8, 128), F32),
            pltpu.VMEM((16, 8, 128), F32),
            pltpu.VMEM((16, 128), F32),
            pltpu.VMEM((32, 8, 128), F32),
            pltpu.VMEM((32, 8, 128), F32),
            pltpu.VMEM((16, 128), F32),
            pltpu.VMEM((NY, 16, 128), F32),
            pltpu.VMEM((16, 128), F32),
            pltpu.VMEM((NX, 16, 128), F32),
            pltpu.VMEM((1, 128), F32),
            pltpu.VMEM((32, 1, 128), F32),
            pltpu.VMEM((1, 128), F32),
            pltpu.VMEM((16, 1, 128), F32),
            pltpu.VMEM((88, 128), F32),
            pltpu.VMEM((4, DIMS, 512), F32),
            pltpu.VMEM((3, NX, DIMS, 128), F32),
            pltpu.VMEM((3, DIMS, 128), F32),
            pltpu.VMEM((3, NY, 8, 128), F32),
            pltpu.VMEM((NY, 8, 512), F32),
            pltpu.VMEM((8, 512), F32),
            pltpu.VMEM((NX, 8, 128), F32),
            pltpu.VMEM((4, 8, 128), F32),
            pltpu.VMEM((4, 80, 256), F32),
            pltpu.VMEM((4, 40, 256), F32),
            pltpu.VMEM((NZ, 40, 128), F32),
            pltpu.VMEM((NZ, 40, 128), F32),
            pltpu.VMEM((32, 128), F32),
            pltpu.VMEM((32, 128), F32),
            pltpu.SemaphoreType.DMA((35,)),
            pltpu.SemaphoreType.DMA((35,)),
            pltpu.SemaphoreType.DMA((22,)),
        ],
        compiler_params=pltpu.CompilerParams(
            collective_id=0, has_side_effects=True, vmem_limit_bytes=60 << 20
        ),
    )(source_cells, target_cells, source_mass.reshape(8, 128), target_mass.reshape(16, 128))
    f, g, smap, tmap = pl.pallas_call(
        finish,
        out_shape=(
            jax.ShapeDtypeStruct((8, 128), F32),
            jax.ShapeDtypeStruct((16, 128), F32),
            jax.ShapeDtypeStruct((DIMS, 64), F32),
            jax.ShapeDtypeStruct((DIMS, TGT), F32),
        ),
        in_specs=[anywhere] * 3,
        out_specs=(anywhere,) * 4,
        scratch_shapes=[
            pltpu.VMEM((24, 128), F32),
            pltpu.VMEM((DIMS, 64), F32),
            pltpu.VMEM((DIMS, TGT), F32),
            pltpu.SemaphoreType.DMA((4,)),
            pltpu.SemaphoreType.DMA((5,)),
        ],
    )(*results)
    return f.reshape(-1), g.reshape(-1), smap, tmap


def solution(mesh):
    in_specs = (P(None, "rows"), P(None, "cols"), P("rows"), P("cols"))
    out_specs = (P("rows"), P("cols"), P(None, ("rows", "cols")), P(None, "cols"))
    return jax.shard_map(local, mesh=mesh, in_specs=in_specs, out_specs=out_specs, check_vma=False)
```

```python
import functools
import math

import jax
import jax.numpy as jnp
from jax import lax
from jax.experimental import pallas as pl
from jax.experimental.pallas import tpu as pltpu
from jax.sharding import PartitionSpec as P

MESH = pl.DeviceIdType.MESH
F32 = jnp.float32
BF16 = jnp.bfloat16
LOG2E = math.log2(math.e)
LN2 = math.log(2.0)
NEG = -3.0e38

DIMS = 64
SRC = 1024
TGT = 2048
NX, NY, NZ, NC = 4, 8, 8, 2
GROUPS = 16


def far(n, r):
    return min(r, n - r)


XY_OFFSETS = sorted(
    [(dy, dx) for dy in range(NY) for dx in range(NX) if dy or dx],
    key=lambda o: -(far(NY, o[0]) + far(NX, o[1])),
)
ZC_OFFSETS = sorted(
    [(dz, dc) for dz in range(NZ) for dc in range(NC) if dz or dc],
    key=lambda o: -(far(NZ, o[0]) + 0.3 * o[1]),
)
Y_OFFSETS = sorted(range(1, NY), key=lambda r: -far(NY, r))
X_OFFSETS = sorted(range(1, NX), key=lambda r: -far(NX, r))
Z_OFFSETS = sorted(range(1, NZ), key=lambda r: -far(NZ, r))


def split3(value):
    high = value.astype(BF16)
    rest = value - high.astype(F32)
    middle = rest.astype(BF16)
    low = (rest - middle.astype(F32)).astype(BF16)
    return high, middle, low


def split2(value):
    high = value.astype(BF16)
    return high, (value - high.astype(F32)).astype(BF16)


def fold_rows(value, op):
    rows = value.shape[0]
    while rows > 8:
        rows //= 2
        value = op(value[:rows], value[rows:])
    return value


def to_row(ref, groups):
    return jnp.concatenate([ref[r : r + 1, :] for r in range(groups)], axis=1)


def from_row(ref, value, groups):
    for r in range(groups):
        ref[r : r + 1, :] = value[:, r * 128 : (r + 1) * 128]


def kernel(
    x_hbm, y_hbm, a_hbm, b_hbm,
    fg_hbm, smap_hbm, tmap_hbm,
    x_ref, y_ref, a_ref, b_ref, fg_ref, smap_ref, tmap_ref,
    xt, yk, t, ehi, elo, fb, part,
    f1_out, f1_in, f2_out, f2_in, g1_out, g1a_in, g1b_in, g2_out, g2y_in, g2_mid, g2x_in,
    sa_out, sa_in, sb_out, sb_in, row,
    tn, ax_in, ra, ay_in, by_in, rb, bx_in, fin_t,
    sn, sc_in, zs, z_in, fin, fin_in,
    send, recv, near,
):
    rows_at, cols_at = lax.axis_index("rows"), lax.axis_index("cols")
    my, mx = rows_at // NX, lax.rem(rows_at, NX)
    mz, mc = cols_at // NC, lax.rem(cols_at, NC)

    def xy(dy, dx):
        return (lax.rem(my + dy, NY) * NX + lax.rem(mx + dx, NX), cols_at)

    def zc(dz, dc):
        return (rows_at, lax.rem(mz + dz, NZ) * NC + lax.rem(mc + dc, NC))

    def push(src, dst, phase, device):
        pltpu.make_async_remote_copy(
            src_ref=src, dst_ref=dst, send_sem=send.at[phase], recv_sem=recv.at[phase],
            device_id=device, device_id_type=MESH,
        ).start()

    def await_bytes(ref, sem):
        pltpu.make_async_copy(ref, ref, sem).wait()

    def push_xy(src, slots, phase):
        for dy, dx in XY_OFFSETS:
            push(src, slots.at[dy * NX + dx], phase, xy(dy, dx))

    def push_zc(src, slots, phase):
        for dz, dc in ZC_OFFSETS:
            push(src, slots.at[dz * NC + dc], phase, zc(dz, dc))

    def fetch(src, dst, k):
        copy = pltpu.make_async_copy(src, dst, near.at[k])
        copy.start()
        return copy

    loads = [
        fetch(x_hbm, x_ref, 0),
        fetch(y_hbm, y_ref, 1),
        fetch(a_hbm, a_ref, 2),
        fetch(b_hbm, b_ref, 3),
    ]
    barrier = pltpu.get_barrier_semaphore()
    for dy, dx in XY_OFFSETS:
        pl.semaphore_signal(barrier, inc=1, device_id=xy(dy, dx), device_id_type=MESH)
    for dz, dc in ZC_OFFSETS:
        pl.semaphore_signal(barrier, inc=1, device_id=zc(dz, dc), device_id_type=MESH)

    loads[0].wait()
    x = x_ref[...]
    xs = x * (4.0 * LOG2E)
    xh, xm, xl = split3(xs)
    xt[:, 0:128] = jnp.concatenate([xh.astype(F32), xm.astype(F32)], axis=0).T.astype(BF16)
    xt[:, 128:256] = xt[:, 0:128]
    xt[:, 256:384] = jnp.concatenate([xh.astype(F32), xl.astype(F32)], axis=0).T.astype(BF16)
    xt[:, 384:512] = jnp.where(lax.broadcasted_iota(jnp.int32, (SRC, 128), 1) < 3, 1.0, 0.0).astype(BF16)
    loads[1].wait()
    y = y_ref[...]
    yh, ym, yl = split3(y)
    yk[0:64, :] = yh
    yk[64:128, :] = yh
    yk[128:192, :] = ym
    yk[192:256, :] = ym
    yk[256:320, :] = yl
    yk[320:384, :] = yh
    ny = jnp.sum(y * y, axis=0, keepdims=True) * (-2.0 * LOG2E)
    nh, nm, nl = split3(ny)
    pick = lax.broadcasted_iota(jnp.int32, (16, TGT), 0)
    norms = jnp.where(
        pick == 0, nh.astype(F32), jnp.where(pick == 1, nm.astype(F32), jnp.where(pick == 2, nl.astype(F32), 0.0))
    )
    yk[384:400, :] = norms.astype(BF16)
    yk[400:512, :] = jnp.zeros((112, TGT), BF16)

    def score(k):
        at = slice(k * 128, (k + 1) * 128)
        t[at, :] = jnp.dot(xt[at, :], yk[...], preferred_element_type=F32)

    def row_logs(k):
        at = slice(k * 128, (k + 1) * 128)
        highest = t[at, 0:128]
        for g in range(1, GROUPS):
            highest = jnp.maximum(highest, t[at, g * 128 : (g + 1) * 128])
        total = jnp.exp2(t[at, 0:128] - highest)
        for g in range(1, GROUPS):
            total += jnp.exp2(t[at, g * 128 : (g + 1) * 128] - highest)
        highest, total = highest.T, total.T
        top = jnp.max(highest, axis=0, keepdims=True)
        summed = jnp.sum(total * jnp.exp2(highest - top), axis=0, keepdims=True)
        f1_out[k : k + 1, :] = top + jnp.log(summed) * LOG2E

    score(0)
    for k in range(8):
        if k < 7:
            score(k + 1)
        row_logs(k)
    loads[2].wait()
    loads[3].wait()
    sa_out[...] = jnp.broadcast_to(jnp.sum(a_ref[...], axis=(0, 1), keepdims=True), (1, 128))
    sb_out[...] = jnp.broadcast_to(jnp.sum(b_ref[...], axis=(0, 1), keepdims=True), (1, 128))

    pl.semaphore_wait(barrier, len(XY_OFFSETS) + len(ZC_OFFSETS))
    push_zc(f1_out, f1_in, 0)
    push_xy(sa_out, sa_in, 1)
    push_zc(sb_out, sb_in, 2)

    f1_in[0] = f1_out[...]
    await_bytes(f1_in.at[pl.ds(1, 15)], recv.at[0])
    highest = jnp.max(f1_in[...], axis=0)
    summed = jnp.sum(jnp.exp2(f1_in[...] - highest[None]), axis=0)
    log_a = jnp.log(a_ref[...]) * LOG2E
    first_f = log_a - (highest + jnp.log(summed) * LOG2E)
    row[0:8, :] = first_f
    for r in range(8):
        fb[r * 128 : (r + 1) * 128, :] = jnp.broadcast_to(row[r : r + 1, :], (128, 128)).T

    WIDE = 512
    for c in range(TGT // WIDE):
        cs = slice(c * WIDE, (c + 1) * WIDE)

        def shifted(k, top):
            at = pl.ds(pl.multiple_of(k * 64, 64), 64)
            f = fb[at, :]
            value = t[at, cs] + jnp.concatenate([f] * (WIDE // 128), axis=1)
            t[at, cs] = value
            return jnp.maximum(top, fold_rows(value, jnp.maximum))

        top = lax.fori_loop(0, 16, shifted, jnp.full((8, WIDE), NEG, F32), unroll=2)
        top = jnp.max(top, axis=0, keepdims=True)

        def powers(k, total):
            at = pl.ds(pl.multiple_of(k * 64, 64), 64)
            e = jnp.exp2(t[at, cs] - top)
            t[at, cs] = e
            high, low = split2(e)
            ehi[at, cs] = high
            elo[at, cs] = low
            return total + fold_rows(e, jnp.add)

        total = lax.fori_loop(0, 16, powers, jnp.zeros((8, WIDE), F32), unroll=2)
        total = jnp.sum(total, axis=0, keepdims=True)
        logs = top + jnp.log(total) * LOG2E
        for r in range(WIDE // 128):
            at = c * (WIDE // 128) + r
            g1_out[at : at + 1, :] = logs[:, r * 128 : (r + 1) * 128]
            row[8 + at : 9 + at, :] = top[:, r * 128 : (r + 1) * 128]
        if c == 1:
            push_xy(g1_out.at[0:8], g1a_in, 3)
    push_xy(g1_out.at[8:16], g1b_in, 4)
    b = b_ref[...]
    log_b = jnp.log(b) * LOG2E

    def log_sum(slots):
        highest = jnp.max(slots[...], axis=0)
        return highest + jnp.log(jnp.sum(jnp.exp2(slots[...] - highest[None]), axis=0)) * LOG2E

    g1a_in[0] = g1_out[0:8, :]
    await_bytes(g1a_in.at[pl.ds(1, 31)], recv.at[3])
    low_logs = log_sum(g1a_in)
    g1b_in[0] = g1_out[8:16, :]
    await_bytes(g1b_in.at[pl.ds(1, 31)], recv.at[4])
    first_g = log_b - jnp.concatenate([low_logs, log_sum(g1b_in)], axis=0)
    row[8:24, :] = jnp.exp2(row[8:24, :] + first_g)
    scale = to_row(row.at[8:24, :], 16)

    def weighted(k, _):
        at = pl.ds(pl.multiple_of(k * 64, 64), 64)
        total = t[at, 0:128] * scale[:, 0:128]
        for g in range(1, GROUPS):
            gs = slice(g * 128, (g + 1) * 128)
            total += t[at, gs] * scale[:, gs]
        part[at, :] = total
        return 0

    lax.fori_loop(0, 16, weighted, 0, unroll=2)
    for r in range(8):
        f2_out[r : r + 1, :] = jnp.sum(part[r * 128 : (r + 1) * 128, :].T, axis=0, keepdims=True)
    push_zc(f2_out, f2_in, 5)
    f2_in[0] = f2_out[...]
    nx = jnp.sum(x * x, axis=0, keepdims=True) * (2.0 * LOG2E)
    from_row(row.at[24:32, :], nx, 8)
    await_bytes(f2_in.at[pl.ds(1, 15)], recv.at[5])
    sums = jnp.sum(f2_in[...], axis=0)
    ratio = a_ref[...] / sums
    row[32:40, :] = ratio
    u = to_row(row.at[32:40, :], 8)

    def stacked(points, weights):
        high, low = split2(points * weights)
        wh, wl = split2(weights)
        tail = lax.broadcasted_iota(jnp.int32, (16, weights.shape[1]), 0)
        pair = jnp.where(tail == 0, wh.astype(F32), jnp.where(tail == 1, wl.astype(F32), 0.0))
        return jnp.concatenate([high, low, pair.astype(BF16)], axis=0)

    def rows_of(dy):
        return pl.ds(pl.multiple_of(lax.rem(my + dy, NY) * 8, 8), 8)

    def cols_of(dx):
        return pl.ds(pl.multiple_of(lax.rem(mx + dx, NX) * 128, 128), 128)

    own_rows, own_cols = rows_of(0), cols_of(0)

    def gather_x(p):
        for dx in X_OFFSETS:
            push(tn.at[p, :, cols_of(dx)], ax_in.at[p, dx], 23 + p, xy(0, dx))

    def scatter_y(p):
        await_bytes(ax_in.at[p, pl.ds(1, 3)], recv.at[23 + p])
        ra[p] = tn[p, :, own_cols] + ax_in[p, 1] + ax_in[p, 2] + ax_in[p, 3]
        for dy in Y_OFFSETS:
            push(ra.at[p, rows_of(dy), :], ay_in.at[p, dy], 26 + p, xy(dy, 0))

    def return_y(p):
        await_bytes(ay_in.at[p, pl.ds(1, 7)], recv.at[26 + p])
        total = ra[p, own_rows, :]
        for k in range(1, NY):
            total += ay_in[p, k]
        fin_t[p] = total / row[pl.ds(56 + mx * 4 + p, 1), :]
        for dy in Y_OFFSETS:
            push(fin_t.at[p], tmap_ref.at[p, own_rows, own_cols], 29 + p, xy(dy, 0))
        tmap_ref[p, own_rows, own_cols] = fin_t[p]

    def return_x(p):
        await_bytes(ay_in.at[p, pl.ds(1, 7)], recv.at[29 + p])
        for dx in X_OFFSETS:
            push(tmap_ref.at[p, :, own_cols], tmap_ref.at[p, :, own_cols], 32 + p, xy(0, dx))

    xu = stacked(x, u)
    for half in range(2):
        for q in range(NX):
            cs = slice(q * 512 + half * 256, q * 512 + half * 256 + 256)
            one = jnp.dot(xu, ehi[:, cs], preferred_element_type=F32)
            two = jnp.dot(xu, elo[:, cs], preferred_element_type=F32)
            w = scale[:, cs]
            sums = (one[0:64] + one[64:128] + two[0:64]) * w
            tn[half * 2, :, q * 128 : (q + 1) * 128] = sums[:, 0:128]
            tn[half * 2 + 1, :, q * 128 : (q + 1) * 128] = sums[:, 128:256]
            mass = (one[128:129] + one[129:130] + two[128:129]) * w
            at = q * 4 + half * 2
            g2_out[at : at + 1, :] = mass[:, 0:128]
            g2_out[at + 1 : at + 2, :] = mass[:, 128:256]
        if half == 0:
            gather_x(0)
            gather_x(1)
    for dy in Y_OFFSETS:
        push(g2_out, g2y_in.at[dy], 6, xy(dy, 0))
    for dy in Y_OFFSETS:
        push(tn.at[3, rows_of(dy), :], by_in.at[dy], 9, xy(dy, 0))
    gather_x(2)

    scatter_y(0)
    g2y_in[0] = g2_out[...]
    await_bytes(g2y_in.at[pl.ds(1, 7)], recv.at[6])
    g2_mid[...] = jnp.sum(g2y_in[...], axis=0)
    for dx in X_OFFSETS:
        push(g2_mid, g2x_in.at[dx], 8, xy(0, dx))
    scatter_y(1)
    scatter_y(2)
    await_bytes(by_in.at[pl.ds(1, 7)], recv.at[9])
    total = tn[3, own_rows, :]
    for k in range(1, NY):
        total += by_in[k]
    rb[...] = total
    for dx in X_OFFSETS:
        push(rb.at[:, cols_of(dx)], bx_in.at[dx], 11, xy(0, dx))

    g2x_in[0] = g2_mid[...]
    await_bytes(g2x_in.at[pl.ds(1, 3)], recv.at[8])
    row[56:72, :] = jnp.sum(g2x_in[...], axis=0)
    ratio_g = b / row[56:72, :]
    row[72:88, :] = row[8:24, :] * ratio_g
    weights = to_row(row.at[72:88, :], 16)

    yq = stacked(y, weights)
    nt = (((1,), (1,)), ((), ()))
    partner = zc(0, 1)
    own_pair = mz // 2
    pairs = [lax.rem(own_pair + k, NZ // 2) for k in (2, 1, 3, 0)]

    def chunk(k):
        rs = pl.ds(pl.multiple_of(pairs[k] * 256, 256), 256)
        one = lax.dot_general(yq, ehi[rs, :], nt, preferred_element_type=F32)
        two = lax.dot_general(yq, elo[rs, :], nt, preferred_element_type=F32)
        sn[k, 0:32, :] = one[0:32] + one[64:96] + two[0:32]
        sn[k, 40:72, :] = one[32:64] + one[96:128] + two[32:64]
        weight = jnp.broadcast_to(one[128:129] + one[129:130] + two[128:129], (8, 256))
        sn[k, 32:40, :] = weight
        sn[k, 72:80, :] = weight
        theirs = pl.ds(pl.multiple_of((1 - mc) * 40, 8), 40)
        push(sn.at[k, theirs], sc_in.at[k], 19 + k, partner)

    def onward(k):
        await_bytes(sc_in.at[k], recv.at[19 + k])
        mine = pl.ds(pl.multiple_of(mc * 40, 8), 40)
        for e in range(2):
            es = slice(e * 128, (e + 1) * 128)
            zs[k * 2 + e] = sn[k, mine, es] + sc_in[k, :, es]
        if k < 3:
            for e in range(2):
                to = pairs[k] * 2 + e
                hops = lax.rem(to - mz + NZ, NZ)
                push(zs.at[k * 2 + e], z_in.at[hops], 15, (rows_at, to * NC + mc))
        else:
            to = own_pair * 2 + 1 - lax.rem(mz, 2)
            hops = lax.rem(to - mz + NZ, NZ)
            push(zs.at[6 + 1 - lax.rem(mz, 2)], z_in.at[hops], 15, (rows_at, to * NC + mc))

    chunk(0)
    chunk(1)
    onward(0)
    return_y(0)
    return_y(1)
    chunk(2)
    onward(1)
    await_bytes(bx_in.at[pl.ds(1, 3)], recv.at[11])
    fin_t[3] = (rb[:, own_cols] + bx_in[1] + bx_in[2] + bx_in[3]) / row[pl.ds(56 + mx * 4 + 3, 1), :]
    for dx in X_OFFSETS:
        push(fin_t.at[3], tmap_ref.at[3, own_rows, own_cols], 14, xy(0, dx))
    tmap_ref[3, own_rows, own_cols] = fin_t[3]
    chunk(3)
    onward(2)
    return_y(2)
    onward(3)

    return_x(0)
    await_bytes(bx_in.at[pl.ds(1, 3)], recv.at[14])
    for dy in Y_OFFSETS:
        push(tmap_ref.at[3, own_rows, :], tmap_ref.at[3, own_rows, :], 16, xy(dy, 0))
    return_x(1)
    return_x(2)

    sa_in[0] = sa_out[...]
    sb_in[0] = sb_out[...]
    await_bytes(sa_in.at[pl.ds(1, 31)], recv.at[1])
    await_bytes(sb_in.at[pl.ds(1, 15)], recv.at[2])
    log_sa = jnp.log(jnp.sum(sa_in[...], axis=0))
    log_sb = jnp.log(jnp.sum(sb_in[...], axis=0))
    fg_ref[0:8, :] = (0.5 * LN2) * (first_f + row[24:32, :]) + 0.5 * jnp.log(ratio) - (log_sa - 0.5 * log_sb)
    fg_ref[8:24, :] = (0.5 * LN2) * first_g + 0.5 * jnp.log(ratio_g) - (log_sb - log_sa)
    stores = [fetch(fg_ref, fg_hbm, 4)]

    await_bytes(z_in.at[pl.ds(1, 7)], recv.at[15])
    total = zs[6 + lax.rem(mz, 2)]
    for k in range(1, NZ):
        total += z_in[k]
    fin[...] = total[0:32] / total[32:33]
    push(fin, fin_in, 18, partner)
    await_bytes(fin_in, recv.at[18])
    mine, other = fin[...], fin_in[...]
    low = jnp.where(mc == 0, mine, other)
    high = jnp.where(mc == 0, other, mine)
    both = jnp.concatenate([low, high], axis=0)
    smap_ref[...] = jnp.where(mc == 0, both[:, 0:64], both[:, 64:128])
    stores.append(fetch(smap_ref, smap_hbm, 5))

    def store(p):
        for q in range(NX):
            place = tmap_hbm.at[:, q * 512 + p * 128 : q * 512 + p * 128 + 128]
            stores.append(fetch(tmap_ref.at[p, :, q * 128 : q * 128 + 128], place, 6 + p * 4 + q))

    await_bytes(ax_in.at[0, pl.ds(1, 3)], recv.at[32])
    store(0)
    await_bytes(ax_in.at[1, pl.ds(1, 3)], recv.at[33])
    store(1)
    await_bytes(by_in.at[pl.ds(1, 7)], recv.at[16])
    store(3)
    await_bytes(ax_in.at[2, pl.ds(1, 3)], recv.at[34])
    store(2)

    await_bytes(f1_in.at[pl.ds(1, 15)], send.at[0])
    await_bytes(sa_in.at[pl.ds(1, 31)], send.at[1])
    await_bytes(sb_in.at[pl.ds(1, 15)], send.at[2])
    await_bytes(g1a_in.at[pl.ds(1, 31)], send.at[3])
    await_bytes(g1b_in.at[pl.ds(1, 31)], send.at[4])
    await_bytes(f2_in.at[pl.ds(1, 15)], send.at[5])
    await_bytes(g2y_in.at[pl.ds(1, 7)], send.at[6])
    await_bytes(g2x_in.at[pl.ds(1, 3)], send.at[8])
    await_bytes(by_in.at[pl.ds(1, 7)], send.at[9])
    await_bytes(bx_in.at[pl.ds(1, 3)], send.at[11])
    for k in range(4):
        await_bytes(sc_in.at[k], send.at[19 + k])
    await_bytes(bx_in.at[pl.ds(1, 3)], send.at[14])
    await_bytes(z_in.at[pl.ds(1, 7)], send.at[15])
    await_bytes(by_in.at[pl.ds(1, 7)], send.at[16])
    for p in range(3):
        await_bytes(ax_in.at[p, pl.ds(1, 3)], send.at[23 + p])
        await_bytes(ay_in.at[p, pl.ds(1, 7)], send.at[26 + p])
        await_bytes(ay_in.at[p, pl.ds(1, 7)], send.at[29 + p])
        await_bytes(ax_in.at[p, pl.ds(1, 3)], send.at[32 + p])
    await_bytes(fin_in, send.at[18])
    for copy in stores:
        copy.wait()


def finish(fg, sm, tm, f_hbm, g_hbm, smap_hbm, tmap_hbm, fg_v, sm_v, tm_v, come, go):
    loads = [pltpu.make_async_copy(tm.at[k * 32 : k * 32 + 32], tm_v.at[k * 32 : k * 32 + 32], come.at[k]) for k in range(2)]
    loads += [pltpu.make_async_copy(sm, sm_v, come.at[2]), pltpu.make_async_copy(fg, fg_v, come.at[3])]
    stores = [pltpu.make_async_copy(tm_v.at[k * 32 : k * 32 + 32], tmap_hbm.at[k * 32 : k * 32 + 32], go.at[k]) for k in range(2)]
    stores += [
        pltpu.make_async_copy(sm_v, smap_hbm, go.at[2]),
        pltpu.make_async_copy(fg_v.at[0:8], f_hbm, go.at[3]),
        pltpu.make_async_copy(fg_v.at[8:24], g_hbm, go.at[4]),
    ]
    for copy in loads:
        copy.start()
    for k, copy in enumerate(loads):
        copy.wait()
        stores[k].start()
    stores[4].start()
    for copy in stores:
        copy.wait()


def local(source_cells, target_cells, source_mass, target_mass):
    anywhere = pl.BlockSpec(memory_space=pl.ANY)
    results = pl.pallas_call(
        kernel,
        out_shape=(
            jax.ShapeDtypeStruct((24, 128), F32),
            jax.ShapeDtypeStruct((DIMS, 64), F32),
            jax.ShapeDtypeStruct((DIMS, TGT), F32),
        ),
        in_specs=[anywhere] * 4,
        out_specs=(anywhere,) * 3,
        scratch_shapes=[
            pltpu.VMEM((DIMS, SRC), F32),
            pltpu.VMEM((DIMS, TGT), F32),
            pltpu.VMEM((8, 128), F32),
            pltpu.VMEM((16, 128), F32),
            pltpu.VMEM((24, 128), F32),
            pltpu.VMEM((DIMS, 64), F32),
            pltpu.VMEM((4, DIMS, 512), F32),
            pltpu.VMEM((SRC, 512), BF16),
            pltpu.VMEM((512, TGT), BF16),
            pltpu.VMEM((SRC, TGT), F32),
            pltpu.VMEM((SRC, TGT), BF16),
            pltpu.VMEM((SRC, TGT), BF16),
            pltpu.VMEM((SRC, 128), F32),
            pltpu.VMEM((SRC, 128), F32),
            pltpu.VMEM((8, 128), F32),
            pltpu.VMEM((16, 8, 128), F32),
            pltpu.VMEM((8, 128), F32),
            pltpu.VMEM((16, 8, 128), F32),
            pltpu.VMEM((16, 128), F32),
            pltpu.VMEM((32, 8, 128), F32),
            pltpu.VMEM((32, 8, 128), F32),
            pltpu.VMEM((16, 128), F32),
            pltpu.VMEM((NY, 16, 128), F32),
            pltpu.VMEM((16, 128), F32),
            pltpu.VMEM((NX, 16, 128), F32),
            pltpu.VMEM((1, 128), F32),
            pltpu.VMEM((32, 1, 128), F32),
            pltpu.VMEM((1, 128), F32),
            pltpu.VMEM((16, 1, 128), F32),
            pltpu.VMEM((88, 128), F32),
            pltpu.VMEM((4, DIMS, 512), F32),
            pltpu.VMEM((3, NX, DIMS, 128), F32),
            pltpu.VMEM((3, DIMS, 128), F32),
            pltpu.VMEM((3, NY, 8, 128), F32),
            pltpu.VMEM((NY, 8, 512), F32),
            pltpu.VMEM((8, 512), F32),
            pltpu.VMEM((NX, 8, 128), F32),
            pltpu.VMEM((4, 8, 128), F32),
            pltpu.VMEM((4, 80, 256), F32),
            pltpu.VMEM((4, 40, 256), F32),
            pltpu.VMEM((NZ, 40, 128), F32),
            pltpu.VMEM((NZ, 40, 128), F32),
            pltpu.VMEM((32, 128), F32),
            pltpu.VMEM((32, 128), F32),
            pltpu.SemaphoreType.DMA((35,)),
            pltpu.SemaphoreType.DMA((35,)),
            pltpu.SemaphoreType.DMA((22,)),
        ],
        compiler_params=pltpu.CompilerParams(
            collective_id=0, has_side_effects=True, vmem_limit_bytes=60 << 20
        ),
    )(source_cells, target_cells, source_mass.reshape(8, 128), target_mass.reshape(16, 128))
    f, g, smap, tmap = pl.pallas_call(
        finish,
        out_shape=(
            jax.ShapeDtypeStruct((8, 128), F32),
            jax.ShapeDtypeStruct((16, 128), F32),
            jax.ShapeDtypeStruct((DIMS, 64), F32),
            jax.ShapeDtypeStruct((DIMS, TGT), F32),
        ),
        in_specs=[anywhere] * 3,
        out_specs=(anywhere,) * 4,
        scratch_shapes=[
            pltpu.VMEM((24, 128), F32),
            pltpu.VMEM((DIMS, 64), F32),
            pltpu.VMEM((DIMS, TGT), F32),
            pltpu.SemaphoreType.DMA((4,)),
            pltpu.SemaphoreType.DMA((5,)),
        ],
    )(*results)
    return f.reshape(-1), g.reshape(-1), smap, tmap


def solution(mesh):
    in_specs = (P(None, "rows"), P(None, "cols"), P("rows"), P("cols"))
    out_specs = (P("rows"), P("cols"), P(None, ("rows", "cols")), P(None, "cols"))
    return jax.shard_map(local, mesh=mesh, in_specs=in_specs, out_specs=out_specs, check_vma=False)
```
